128 devices in a mesh: band: 4 (over y), grid: 32 (over z, x, core).
Axes of the slice: x: 4, y: 4, z: 4, core: 2. Of those that a mesh axis runs over, the one named last changes fastest.
Arguments:
- orbitals: float32 [2, 8, 256, 256, 256], P(None, 'band', 'grid'), may hold values from -6 to 6
- potential: float32 [256, 256, 256], P('grid'), may hold values from -6 to 6
- projectors: float32 [4, 16384, 128], P(None, 'grid'), may hold values from -0.375 to 0.375
- entry_atom: int32 [16384], P('grid'), may hold values from 0 to 511
- entry_block: int32 [16384], P('grid'), may hold values from 0 to 4095
- entry_count: int32 [16384], P('grid'), may hold values from 1 to 128
- owner_slot: int32 [512], replicated, may hold values from 0 to 511, each once
- strength: float32 [512], replicated, may hold values from 0.1 to 1
Outputs:
- propagated: float32 [2, 8, 256, 256, 256], P(None, 'band', 'grid')
- density: float32 [256, 256, 256], P('grid')
- forces: float32 [3, 512], P(None, 'grid')
The draws below stay inside these ranges and needn't reach their ends.
Inputs may be any that keep to these rules, and one draw needn't show every extreme that they name: `owner_slot`: a permutation: owner slot s belongs to grid device s // 16.
All inputs are finite; a program needn't handle non-finite values.
Results may differ from the reference program's by a relative error of at most 0.00013.
Values sent between devices are 32-bit elements; how exact they have to be, the bound alone decides.
No kernel may reach another device: no remote copies, remote signals or barrier semaphores. Data moves between devices by JAX's collectives and lax.ppermute only.
A program may use at most 128 MiB of HBM per device.

```python
import math
import jax
import jax.numpy as jnp
import numpy as np
from jax import lax

NX = 256
NY = 256
NZ = 256
BLOCK = 128
BLK_DEV = 512
NB = 8
ENTRIES = 16384
ATOMS = 512
BLOCKS_DEV = 4096


def set_ends(values, stream_key, least, largest):
    shape = values.shape
    index_at = [jax.random.randint(jax.random.fold_in(stream_key, axis), (), 0, shape[axis]) for axis in range(len(shape))]
    values = values.at[tuple(index_at)].set(least)
    longest = shape.index(max(shape))
    index_at[longest] = (index_at[longest] + 1) % shape[longest]
    return values.at[tuple(index_at)].set(largest)


def block_levels(own_key, dims, pieces, smallest, largest):
    gain, own = 1.0, jax.random.fold_in(own_key, 6)
    for position, parts in pieces:
        draws = jnp.exp(jax.random.uniform(jax.random.fold_in(own, position), (parts,), jnp.float32, smallest / len(pieces), largest / len(pieces)))
        gain = gain * jnp.repeat(draws, dims[position] // parts).reshape([-1 if axis == position else 1 for axis in range(len(dims))])
    return gain


def cumulative_ranks(number_of, skew):
    loads = [(1 << 20) // math.isqrt(grade ** skew) + 1 for grade in range(1, number_of + 1)]
    spread = 1 + sum(loads) // (1 << 30)
    return np.cumsum(np.array([max(1, weight // spread) for weight in loads]))


def ranked(rng, dims, number_of, skew):
    table = cumulative_ranks(number_of, skew)
    pick = jax.random.randint(jax.random.fold_in(rng, 1), dims, 0, int(table[number_of - 1]))
    standing = jnp.searchsorted(jnp.asarray(table, jnp.int32), pick, side="right")
    return jax.random.permutation(jax.random.fold_in(rng, 2), number_of)[standing].astype(jnp.int32)


def scatter_about(stream_key, extent, width, limit, cuts=(), kind=jnp.bfloat16):
    array = jax.random.normal(stream_key, extent, jnp.float32) * width
    if len(cuts) > 0:
        array = block_levels(stream_key, extent, cuts, -0.22, 0.18) * array
    return jnp.clip(array, min=-limit, max=limit).astype(kind)


def setup_inputs(seed: int = 0) -> dict:
    splits = jax.random.split(jax.random.key(seed), 9)
    orbitals = scatter_about(splits[0], (2, NB, NX, NY, NZ), 1.0, 6.0, ((1, 4), (2, 32)), jnp.float32)
    potential = scatter_about(splits[1], (NX, NY, NZ), 1.0, 6.0, ((0, 32),), jnp.float32)
    projectors = scatter_about(splits[2], (4, ENTRIES, BLOCK), 256 ** -0.5, 0.375, ((1, 32),), jnp.float32)
    entry_atom = set_ends(ranked(splits[3], (ENTRIES,), ATOMS, 2), jax.random.fold_in(splits[3], 3), 0, ATOMS - 1).astype(jnp.int32)
    entry_block = set_ends(jax.random.randint(splits[4], (ENTRIES,), 0, BLOCKS_DEV), jax.random.fold_in(splits[4], 1), 0, BLOCKS_DEV - 1).astype(jnp.int32)
    entry_count = set_ends(jax.random.randint(splits[5], (ENTRIES,), 1, BLOCK + 1), jax.random.fold_in(splits[5], 1), 1, BLOCK).astype(jnp.int32)
    owner_slot = jax.random.permutation(splits[6], ATOMS).astype(jnp.int32)
    strength = jnp.clip(jnp.exp(jax.random.uniform(splits[7], (ATOMS,), jnp.float32, math.log(0.1), math.log(1.0))), 0.1, 1.0)
    return {"orbitals": orbitals, "potential": potential, "projectors": projectors, "entry_atom": entry_atom, "entry_block": entry_block, "entry_count": entry_count, "owner_slot": owner_slot, "strength": strength}


TIME_STEP = 4.0
HIGHEST = lax.Precision.HIGHEST


def wave_square(size):
    index = jnp.arange(size, dtype=jnp.int32)
    freq = jnp.where(index < size // 2, index, index - size).astype(jnp.float32)
    wave = freq * (2.0 * math.pi / size)
    return wave * wave


def turn(real_part, imag_part, cosine, sine):
    return cosine * real_part + sine * imag_part, cosine * imag_part - sine * real_part


def couple(values, strength):
    theta = TIME_STEP * strength
    less_one = jnp.cos(theta) - 1.0
    sine = jnp.sin(theta)
    return jnp.stack([less_one * values[0] + sine * values[1], less_one * values[1] - sine * values[0]])


def reference(orbitals, potential, projectors, entry_atom, entry_block, entry_count, owner_slot, strength):
    angle = (0.5 * TIME_STEP) * potential
    cosine = jnp.cos(angle)
    sine = jnp.sin(angle)
    real_part, imag_part = turn(orbitals[0], orbitals[1], cosine, sine)
    shifted = jnp.stack([real_part, imag_part])
    flat = shifted.reshape(2, NB, NX * NY * NZ // BLOCK, BLOCK)
    entries = jnp.arange(ENTRIES, dtype=jnp.int32)
    global_block = (entries // BLK_DEV) * BLOCKS_DEV + entry_block
    points = jnp.arange(BLOCK, dtype=jnp.int32)
    masked = projectors * (points[None, :] < entry_count[:, None]).astype(jnp.float32)[None]
    gathered = flat[:, :, global_block, :]
    intersections = jnp.einsum("fep,coep->fcoe", masked, gathered, precision=HIGHEST)
    entry_slot = owner_slot[entry_atom]
    sums = jax.ops.segment_sum(jnp.transpose(intersections, (3, 0, 1, 2)), entry_slot, num_segments=ATOMS)
    sums = jnp.transpose(sums, (1, 2, 3, 0))
    coefficients = couple(sums[0], strength)
    forces = -2.0 * strength * jnp.sum(sums[0][None] * sums[1:], axis=(1, 2))
    per_entry = coefficients[:, :, entry_slot]
    flat = flat.at[:, :, global_block, :].add(per_entry[..., None] * masked[0][None, None])
    field = flat.reshape(2, NB, NX, NY, NZ)
    spectrum = jnp.fft.fftn(lax.complex(field[0], field[1]), axes=(1, 2, 3))
    kinetic = (0.5 * TIME_STEP) * (wave_square(NX)[:, None, None] + wave_square(NY)[None, :, None] + wave_square(NZ)[None, None, :])
    spec_real, spec_imag = turn(jnp.real(spectrum), jnp.imag(spectrum), jnp.cos(kinetic), jnp.sin(kinetic))
    moved = jnp.fft.ifftn(lax.complex(spec_real, spec_imag), axes=(1, 2, 3))
    real_part, imag_part = turn(jnp.real(moved), jnp.imag(moved), cosine, sine)
    density = jnp.sum(real_part * real_part + imag_part * imag_part, axis=0)
    return jnp.stack([real_part, imag_part]), density, forces
```

```python
import functools
import math

import jax
import jax.numpy as jnp
import ml_dtypes
import numpy as np
from jax import lax
from jax.experimental import pallas as pl
from jax.experimental.pallas import tpu as pltpu
from jax.sharding import PartitionSpec as P

SIZE = 256
HALF = SIZE // 2
LANES = 128
TIME_STEP = 4.0
HIGHEST = lax.Precision.HIGHEST
ORBS = 2
PLANES = 8
GROUPS = 32
ENTRIES = 512
ATOMS = 512
FIRST = 6
MIB = 1 << 20


def propagator_tables():
    index = np.arange(SIZE)
    freq = np.where(index < HALF, index, index - SIZE)
    wave = freq * (2.0 * math.pi / SIZE)
    line = np.fft.ifft(np.exp(-0.5j * TIME_STEP * wave * wave))
    full = line[(index[:, None] - index[None, :]) % SIZE]
    parts = []
    for sign in (1.0, -1.0):
        half = 0.5 * (full[:HALF, :HALF] + sign * full[:HALF, HALF:])
        real = np.block([[half.real, -half.imag], [half.imag, half.real]]).astype(np.float32)
        high = real.astype(ml_dtypes.bfloat16)
        low = (real - high.astype(np.float32)).astype(ml_dtypes.bfloat16)
        parts += [high, low]
    left = np.stack(parts)
    return left, np.ascontiguousarray(np.swapaxes(left, 1, 2))


def cos_sin(angle):
    turns = jnp.floor(angle * (2.0 / math.pi) + 0.5)
    rest = angle - turns * 1.5703125
    rest = rest - turns * 4.837512969970703125e-4
    rest = rest - turns * 7.54978995489188216e-8
    square = rest * rest
    sine = ((-1.9515295891e-4 * square + 8.3321608736e-3) * square - 1.6666654611e-1) * square * rest + rest
    cosine = ((2.443315711809948e-5 * square - 1.388731625493765e-3) * square + 4.166664568298827e-2) * (
        square * square
    ) - 0.5 * square + 1.0
    quarter = turns.astype(jnp.int32)
    odd = (quarter & 1) == 1
    cos_out = jnp.where(odd, sine, cosine)
    sin_out = jnp.where(odd, cosine, sine)
    cos_out = jnp.where(((quarter + 1) & 2) == 2, -cos_out, cos_out)
    sin_out = jnp.where((quarter & 2) == 2, -sin_out, sin_out)
    return cos_out, sin_out


def two_parts(values):
    high = values.astype(jnp.bfloat16)
    low = (values - high.astype(jnp.float32)).astype(jnp.bfloat16)
    return high, low


def three_parts(values):
    high = values.astype(jnp.bfloat16)
    rest = values - high.astype(jnp.float32)
    middle = rest.astype(jnp.bfloat16)
    low = (rest - middle.astype(jnp.float32)).astype(jnp.bfloat16)
    return jnp.concatenate([high, middle, low], axis=0)


def dot(left, right):
    return jnp.dot(left, right, preferred_element_type=jnp.float32)


def left_product(table, at, values):
    high, low = two_parts(values)
    return dot(table[at], high) + dot(table[at], low) + dot(table[at + 1], high)


def right_product(table, at, values):
    high, low = two_parts(values)
    return dot(high, table[at]) + dot(low, table[at]) + dot(high, table[at + 1])


def propagate_rows(table, real, imag):
    plus = jnp.concatenate([real[:HALF] + real[HALF:], imag[:HALF] + imag[HALF:]], axis=0)
    minus = jnp.concatenate([real[:HALF] - real[HALF:], imag[:HALF] - imag[HALF:]], axis=0)
    plus = left_product(table, 0, plus)
    minus = left_product(table, 2, minus)
    low, high = plus + minus, plus - minus
    return (
        jnp.concatenate([low[:HALF], high[:HALF]], axis=0),
        jnp.concatenate([low[HALF:], high[HALF:]], axis=0),
    )


def propagate_lanes(table, real, imag):
    plus = jnp.concatenate([real[0] + real[1], imag[0] + imag[1]], axis=1)
    minus = jnp.concatenate([real[0] - real[1], imag[0] - imag[1]], axis=1)
    plus = right_product(table, 0, plus)
    minus = right_product(table, 2, minus)
    low, high = plus + minus, plus - minus
    return (
        jnp.concatenate([low[:, :HALF], high[:, :HALF]], axis=1),
        jnp.concatenate([low[:, HALF:], high[:, HALF:]], axis=1),
    )


def atom_matrix(atom_ref):
    atoms = lax.broadcasted_iota(jnp.int32, (ATOMS, ENTRIES), 0)
    return jnp.where(atoms == atom_ref[...], 1.0, 0.0).astype(jnp.bfloat16)


def project_kernel(
    block, count, atom_ref, orbs_hbm, potential_hbm, projectors, sent, partial_ref, masked_ref,
    orbs, potential, rows, counts, table, packed, sems,
):
    half_rows = PLANES * SIZE

    def load(source, into, sem):
        return [
            pltpu.make_async_copy(
                source.at[:, pl.ds(z * LANES, LANES)], into.at[pl.ds(z * half_rows, half_rows)], sem.at[z]
            )
            for z in range(2)
        ]

    copies = [load(potential_hbm, potential, sems.at[4])]
    copies += [load(orbs_hbm.at[k], orbs.at[k], sems.at[k]) for k in range(4)]
    for pair in copies:
        for copy in pair:
            copy.start()

    def arrived(pair):
        for copy in pair:
            copy.wait()

    def place(entry):
        at = block[entry]
        return (at & 1) * half_rows + lax.shift_right_logical(at, 1)

    arrived(copies[0])

    def first(entry, carry):
        rows[4, pl.ds(entry, 1), :] = potential[pl.ds(place(entry), 1), :]
        counts[pl.ds(entry, 1), :] = jnp.full((1, LANES), count[entry], jnp.int32)
        return carry

    lax.fori_loop(0, ENTRIES, first, 0, unroll=8)
    for k in range(4):
        arrived(copies[k + 1])

        def step(entry, carry):
            rows[k, pl.ds(entry, 1), :] = orbs[k, pl.ds(place(entry), 1), :]
            return carry

        lax.fori_loop(0, ENTRIES, step, 0, unroll=8)

    piece = 64

    def reduce(index, carry):
        at = pl.ds(pl.multiple_of(index * piece, piece), piece)
        lane = lax.broadcasted_iota(jnp.int32, (piece, LANES), 1)
        cosine, sine = cos_sin((0.5 * TIME_STEP) * rows[4, at, :])
        inside = lane < counts[at, :]
        fields = []
        for n in range(ORBS):
            real, imag = rows[n, at, :], rows[ORBS + n, at, :]
            fields += [(n, cosine * real + sine * imag), (ORBS + n, cosine * imag - sine * real)]
        out = jnp.zeros((piece, LANES), jnp.float32)
        for f in range(4):
            masked = jnp.where(inside, projectors[f, at, :], 0.0)
            if f == 0:
                masked_ref[at, :] = masked
            for k, field in fields:
                total = jnp.sum(masked * field, axis=1, keepdims=True)
                out = jnp.where(lane == f * 4 + k, total, out)
        table[at, :] = out
        return carry

    lax.fori_loop(0, ENTRIES // piece, reduce, 0)
    turned = jnp.transpose(table[...])[:16]
    sums = lax.dot_general(
        three_parts(turned), atom_matrix(atom_ref), (((1,), (1,)), ((), ())), preferred_element_type=jnp.float32
    )
    sums = sums[:16] + sums[16:32] + sums[32:]
    partial_ref[...] = sums
    for k in range(4):
        for q in range(4):
            packed[k * 4 + q : k * 4 + q + 1, :] = sums[k : k + 1, q * LANES : (q + 1) * LANES]
    for d in range(GROUPS):
        sent[d] = packed[...]


def project(orbs, potential, projectors, entry_atom, entry_block, entry_count):
    smem = pl.BlockSpec(memory_space=pltpu.SMEM)
    vmem = pl.BlockSpec(memory_space=pltpu.VMEM)
    hbm = pl.BlockSpec(memory_space=pl.ANY)
    rows = PLANES * SIZE
    return pl.pallas_call(
        project_kernel,
        out_shape=(
            jax.ShapeDtypeStruct((GROUPS, 16, LANES), jnp.float32),
            jax.ShapeDtypeStruct((16, ATOMS), jnp.float32),
            jax.ShapeDtypeStruct((ENTRIES, LANES), jnp.float32),
        ),
        in_specs=[smem, smem, vmem, hbm, hbm, vmem],
        out_specs=(vmem, vmem, vmem),
        scratch_shapes=[
            pltpu.VMEM((4, 2 * rows, LANES), jnp.float32),
            pltpu.VMEM((2 * rows, LANES), jnp.float32),
            pltpu.VMEM((5, ENTRIES, LANES), jnp.float32),
            pltpu.VMEM((ENTRIES, LANES), jnp.int32),
            pltpu.VMEM((ENTRIES, LANES), jnp.float32),
            pltpu.VMEM((16, LANES), jnp.float32),
            pltpu.SemaphoreType.DMA((5, 2)),
        ],
        compiler_params=pltpu.CompilerParams(vmem_limit_bytes=32 * MIB),
        cost_estimate=pl.CostEstimate(flops=10**9, bytes_accessed=36 * 10**6, transcendentals=0),
        name="project",
    )(entry_block, entry_count, entry_atom.reshape(1, ENTRIES), orbs, potential, projectors)


SHIFT_STEP = 4


def shift_kernel(orbs, potential, first, second):
    for x in range(PLANES):
        cosine, sine = cos_sin((0.5 * TIME_STEP) * potential[x])
        for n, out in enumerate((first, second)):
            real, imag = orbs[0, n, x], orbs[1, n, x]
            both = (cosine * real + sine * imag, cosine * imag - sine * real)
            for c in range(2):
                for d in range(SHIFT_STEP):
                    for z in range(2):
                        tile = both[c][d * 8 : d * 8 + 8, z * LANES : (z + 1) * LANES]
                        out[d, pl.ds(c * 128 + z * 64 + x, 8, stride=8), :] = tile


def shift(orbitals, potential):
    width = SHIFT_STEP * 8
    shape = jax.ShapeDtypeStruct((GROUPS, 256, LANES), jnp.float32)
    spec = pl.BlockSpec((SHIFT_STEP, 256, LANES), lambda i: (i, 0, 0))
    return pl.pallas_call(
        shift_kernel,
        grid=(GROUPS // SHIFT_STEP,),
        out_shape=(shape, shape),
        in_specs=[
            pl.BlockSpec((2, ORBS, PLANES, width, SIZE), lambda i: (0, 0, 0, i, 0)),
            pl.BlockSpec((PLANES, width, SIZE), lambda i: (0, i, 0)),
        ],
        out_specs=(spec, spec),
        compiler_params=pltpu.CompilerParams(vmem_limit_bytes=32 * MIB),
        cost_estimate=pl.CostEstimate(flops=10**8, bytes_accessed=19 * 10**6, transcendentals=0),
        name="shift",
    )(orbitals, potential)


def correct_kernel(n, place, received, strength, atom_ref, masked, before, after, field, coefs, updates, sems):
    load = pltpu.make_async_copy(before, field, sems.at[0])
    load.start()
    sums = jnp.sum(received[...], axis=0)
    real = sums[n * 4 : n * 4 + 4]
    imag = sums[(ORBS + n) * 4 : (ORBS + n) * 4 + 4]
    cosine, sine = cos_sin(TIME_STEP * strength[...])
    less_one = cosine - 1.0
    both = (less_one * real + sine * imag, less_one * imag - sine * real)
    coefs[...] = jnp.zeros_like(coefs)
    for c in range(2):
        for q in range(4):
            coefs[c : c + 1, q * LANES : (q + 1) * LANES] = both[c][q : q + 1]
    spread = dot(three_parts(coefs[...]), atom_matrix(atom_ref))
    spread = jnp.transpose(spread[:16] + spread[16:32] + spread[32:])
    for c in range(2):
        updates[c] = spread[:, c : c + 1] * masked[...]
    load.wait()

    def step(entry, carry):
        row = place[entry]
        for c in range(2):
            at = pl.ds(row + c * 128, 1)
            field[at, :] = field[at, :] + updates[c, pl.ds(entry, 1), :]
        return carry

    lax.fori_loop(0, ENTRIES, step, 0, unroll=8)
    store = pltpu.make_async_copy(field, after, sems.at[1])
    store.start()
    store.wait()


def correct(n, place, received, strength, atoms, masked, before):
    smem = pl.BlockSpec(memory_space=pltpu.SMEM)
    vmem = pl.BlockSpec(memory_space=pltpu.VMEM)
    hbm = pl.BlockSpec(memory_space=pl.ANY)
    return pl.pallas_call(
        functools.partial(correct_kernel, n),
        out_shape=jax.ShapeDtypeStruct((GROUPS * 256, LANES), jnp.float32),
        in_specs=[smem, vmem, vmem, vmem, vmem, hbm],
        out_specs=hbm,
        scratch_shapes=[
            pltpu.VMEM((GROUPS * 256, LANES), jnp.float32),
            pltpu.VMEM((16, ATOMS), jnp.float32),
            pltpu.VMEM((2, ENTRIES, LANES), jnp.float32),
            pltpu.SemaphoreType.DMA((2,)),
        ],
        input_output_aliases={5: 0},
        compiler_params=pltpu.CompilerParams(vmem_limit_bytes=24 * MIB),
        cost_estimate=pl.CostEstimate(flops=5 * 10**8, bytes_accessed=20 * 10**6, transcendentals=0),
        name=f"correct{n}",
    )(place, received, strength, atoms, masked, before.reshape(GROUPS * 256, LANES))


def lines_kernel(n, field, left, right, *rest):
    head, tail, turned, sems = rest[-4:]
    y = pl.program_id(0)
    real = [field[:, 0, z, 0].reshape(SIZE, LANES) for z in range(2)]
    imag = [field[:, 1, z, 0].reshape(SIZE, LANES) for z in range(2)]
    real, imag = propagate_lanes(right, real, imag)
    both = propagate_rows(left, real, imag)
    for c in range(2):
        for z in range(2):
            for d in range(GROUPS):
                tile = both[c][d * 8 : d * 8 + 8, z * LANES : (z + 1) * LANES]
                turned[d, c, z, pl.ds(y, 8, stride=8), :] = tile

    @pl.when(y == pl.num_programs(0) - 1)
    def _():
        cut = FIRST * 8
        copies = [
            pltpu.make_async_copy(turned.at[:, :, :, pl.ds(0, cut)], head.at[:, :, n], sems.at[0]),
            pltpu.make_async_copy(turned.at[:, :, :, pl.ds(cut, 64 - cut)], tail.at[:, :, n], sems.at[1]),
        ]
        for copy in copies:
            copy.start()
        for copy in copies:
            copy.wait()


def lines(n, field, left, right, *before):
    hbm = pl.BlockSpec(memory_space=pl.ANY)
    table = pl.BlockSpec((4, SIZE, SIZE), lambda i: (0, 0, 0))
    return pl.pallas_call(
        functools.partial(lines_kernel, n),
        grid=(8,),
        out_shape=(
            jax.ShapeDtypeStruct((GROUPS, 2, ORBS, 2, FIRST * 8, LANES), jnp.float32),
            jax.ShapeDtypeStruct((GROUPS, 2, ORBS, 2, (PLANES - FIRST) * 8, LANES), jnp.float32),
        ),
        in_specs=[
            pl.BlockSpec((GROUPS, 2, 2, 1, 8, LANES), lambda i: (0, 0, 0, i, 0, 0)),
            table,
            table,
            *[hbm for _ in before],
        ],
        out_specs=(hbm, hbm),
        scratch_shapes=[
            pltpu.VMEM((GROUPS, 2, 2, 64, LANES), jnp.float32),
            pltpu.SemaphoreType.DMA((2,)),
        ],
        input_output_aliases={3 + k: k for k in range(len(before))},
        compiler_params=pltpu.CompilerParams(vmem_limit_bytes=32 * MIB),
        cost_estimate=pl.CostEstimate(flops=5 * 10**9, bytes_accessed=10 * 10**6, transcendentals=0),
        name=f"lines{n}",
    )(field.reshape(GROUPS, 2, 2, 8, 8, LANES), left, right, *before)


def finish_kernel(field, potential, left, *rest):
    out, density = rest[-2:]
    cosine, sine = cos_sin((0.5 * TIME_STEP) * potential[0])
    total = None
    for n in range(ORBS):
        real, imag = (
            jnp.concatenate([field[:, c, n, z].reshape(SIZE, LANES) for z in range(2)], axis=1) for c in range(2)
        )
        real, imag = propagate_rows(left, real, imag)
        real, imag = cosine * real + sine * imag, cosine * imag - sine * real
        out[0, n, 0] = real
        out[1, n, 0] = imag
        square = real * real + imag * imag
        total = square if total is None else total + square
    density[0] = total


def finish(planes, begin, field, potential, left, *before):
    hbm = pl.BlockSpec(memory_space=pl.ANY)
    return pl.pallas_call(
        finish_kernel,
        grid=(planes,),
        out_shape=(
            jax.ShapeDtypeStruct((2, ORBS, PLANES, SIZE, SIZE), jnp.float32),
            jax.ShapeDtypeStruct((planes, SIZE, SIZE), jnp.float32),
        ),
        in_specs=[
            pl.BlockSpec((GROUPS, 2, ORBS, 2, 8, LANES), lambda i: (0, 0, 0, 0, i, 0)),
            pl.BlockSpec((1, SIZE, SIZE), lambda i: (i + begin, 0, 0)),
            pl.BlockSpec((4, SIZE, SIZE), lambda i: (0, 0, 0)),
            *[hbm for _ in before],
        ],
        out_specs=(
            pl.BlockSpec((2, ORBS, 1, SIZE, SIZE), lambda i: (0, 0, i + begin, 0, 0)),
            pl.BlockSpec((1, SIZE, SIZE), lambda i: (i, 0, 0)),
        ),
        input_output_aliases={3 + k: k for k in range(len(before))},
        compiler_params=pltpu.CompilerParams(vmem_limit_bytes=32 * MIB),
        cost_estimate=pl.CostEstimate(flops=10**9 * planes, bytes_accessed=3 * 10**6 * planes, transcendentals=0),
        name=f"finish{begin}",
    )(field, potential, left, *before)


def exchange(array):
    return lax.all_to_all(array, "grid", split_axis=0, concat_axis=0, tiled=True)


def body(left, right, orbitals, potential, projectors, entry_atom, entry_block, entry_count, owner_slot, strength):
    atom_ids = jnp.arange(ATOMS, dtype=jnp.int32)
    rows = PLANES * SIZE
    sent, partials, masked = project(
        orbitals.reshape(2 * ORBS, rows, SIZE), potential.reshape(rows, SIZE), projectors,
        entry_atom, entry_block, entry_count,
    )
    received = exchange(sent)
    shifted = shift(orbitals, potential)
    x, y, z = entry_block // 512, (entry_block // 2) % SIZE, entry_block % 2
    place = (y // 8) * 256 + z * 64 + (y % 8) * 8 + x
    in_slot = owner_slot[:, None] == atom_ids[None, :]
    strength_atom = jnp.sum(jnp.where(in_slot, strength[None, :], 0.0), axis=1).reshape(4, LANES)
    atoms = entry_atom.reshape(1, ENTRIES)
    pencils = [
        exchange(correct(n, place, received, strength_atom, atoms, masked, shifted[n]).reshape(GROUPS, 256, LANES))
        for n in range(ORBS)
    ]
    in_slots = jnp.einsum("ka,as->ks", partials, in_slot.astype(jnp.float32), precision=HIGHEST)
    owned = ATOMS // GROUPS
    mine = lax.psum_scatter(in_slots, "grid", scatter_dimension=1, tiled=True).reshape(4, 2 * ORBS, owned)
    strength_mine = lax.dynamic_slice_in_dim(strength, lax.axis_index("grid") * owned, owned)
    force_local = -2.0 * strength_mine * jnp.sum(mine[0][None] * mine[1:], axis=1)
    forces = lax.psum(force_local, "band")

    back = lines(0, pencils[0], left, right)
    back = lines(1, pencils[1], left, right, *back)
    head = exchange(back[0])
    tail = exchange(back[1])
    out, density_head = finish(FIRST, 0, head, potential, left)
    out, density_tail = finish(PLANES - FIRST, FIRST, tail, potential, left, out)
    density = jnp.concatenate([lax.psum(density_head, "band"), lax.psum(density_tail, "band")], axis=0)
    return out, density, forces


def solution(mesh):
    left, right = propagator_tables()
    in_specs = (
        P(None, "band", "grid", None, None),
        P("grid", None, None),
        P(None, "grid", None),
        P("grid"),
        P("grid"),
        P("grid"),
        P(),
        P(),
    )
    out_specs = (P(None, "band", "grid", None, None), P("grid", None, None), P(None, "grid"))

    def run(*args):
        return body(jnp.asarray(left), jnp.asarray(right), *args)

    return jax.shard_map(run, mesh=mesh, in_specs=in_specs, out_specs=out_specs, check_vma=False)
```

```python
import functools
import math

import jax
import jax.numpy as jnp
import ml_dtypes
import numpy as np
from jax import lax
from jax.experimental import pallas as pl
from jax.experimental.pallas import tpu as pltpu
from jax.sharding import PartitionSpec as P

SIZE = 256
HALF = SIZE // 2
LANES = 128
TIME_STEP = 4.0
HIGHEST = lax.Precision.HIGHEST
ORBS = 2
BANDS = 4
PLANES = 8
GROUPS = 32
ENTRIES = 512
ATOMS = 512
OWNED = ATOMS // GROUPS
CHUNKS = (5, 3)
VMEM = 56 << 20
SENT = 24


def propagator_tables():
    index = np.arange(SIZE)
    freq = np.where(index < HALF, index, index - SIZE)
    wave = freq * (2.0 * math.pi / SIZE)
    line = np.fft.ifft(np.exp(-0.5j * TIME_STEP * wave * wave))
    full = line[(index[:, None] - index[None, :]) % SIZE]
    left = []
    for sign in (1.0, -1.0):
        half = 0.5 * (full[:HALF, :HALF] + sign * full[:HALF, HALF:])
        real = np.block([[half.real, -half.imag], [half.imag, half.real]]).astype(np.float32)
        high = real.astype(ml_dtypes.bfloat16)
        low = (real - high.astype(np.float32)).astype(ml_dtypes.bfloat16)
        left.append(np.concatenate([high, high, low], axis=1))
    left = np.stack(left)
    return left, np.ascontiguousarray(np.swapaxes(left, 1, 2))


def cos_sin(angle):
    turns = jnp.floor(angle * (2.0 / math.pi) + 0.5)
    rest = angle - turns * 1.5703125
    rest = rest - turns * 4.837512969970703125e-4
    rest = rest - turns * 7.54978995489188216e-8
    square = rest * rest
    sine = ((-1.9515295891e-4 * square + 8.3321608736e-3) * square - 1.6666654611e-1) * square * rest + rest
    cosine = ((2.443315711809948e-5 * square - 1.388731625493765e-3) * square + 4.166664568298827e-2) * (
        square * square
    ) - 0.5 * square + 1.0
    quarter = turns.astype(jnp.int32)
    odd = (quarter & 1) == 1
    cos_out = jnp.where(odd, sine, cosine)
    sin_out = jnp.where(odd, cosine, sine)
    cos_out = jnp.where(((quarter + 1) & 2) == 2, -cos_out, cos_out)
    sin_out = jnp.where((quarter & 2) == 2, -sin_out, sin_out)
    return cos_out, sin_out


def split(values, axis):
    high = values.astype(jnp.bfloat16)
    low = (values - high.astype(jnp.float32)).astype(jnp.bfloat16)
    return jnp.concatenate([high, low, high], axis=axis)


def three_parts(values):
    high = values.astype(jnp.bfloat16)
    rest = values - high.astype(jnp.float32)
    middle = rest.astype(jnp.bfloat16)
    low = (rest - middle.astype(jnp.float32)).astype(jnp.bfloat16)
    return jnp.concatenate([high, middle, low], axis=0)


def dot(left, right):
    return jnp.dot(left, right, preferred_element_type=jnp.float32)


def propagate_rows(table, real, imag):
    plus = jnp.concatenate([real[:HALF] + real[HALF:], imag[:HALF] + imag[HALF:]], axis=0)
    minus = jnp.concatenate([real[:HALF] - real[HALF:], imag[:HALF] - imag[HALF:]], axis=0)
    plus = dot(table[0], split(plus, 0))
    minus = dot(table[1], split(minus, 0))
    low, high = plus + minus, plus - minus
    return (
        jnp.concatenate([low[:HALF], high[:HALF]], axis=0),
        jnp.concatenate([low[HALF:], high[HALF:]], axis=0),
    )


def propagate_lanes(table, real, imag):
    plus = jnp.concatenate([real[0] + real[1], imag[0] + imag[1]], axis=1)
    minus = jnp.concatenate([real[0] - real[1], imag[0] - imag[1]], axis=1)
    plus = dot(split(plus, 1), table[0])
    minus = dot(split(minus, 1), table[1])
    low, high = plus + minus, plus - minus
    return (
        jnp.concatenate([low[:, :HALF], high[:, :HALF]], axis=1),
        jnp.concatenate([low[:, HALF:], high[:, HALF:]], axis=1),
    )


def atom_matrix(atom_ref):
    atoms = lax.broadcasted_iota(jnp.int32, (ATOMS, ENTRIES), 0)
    return jnp.where(atoms == atom_ref[...], 1.0, 0.0).astype(jnp.bfloat16)


def project_kernel(
    block, count, atom_ref, slot_ref, orbs_hbm, potential_hbm, projectors, sent, masked_ref,
    orbs, potential, rows, counts, table, packed, sems,
):
    half_rows = PLANES * SIZE

    def load(source, into, sem):
        return [
            pltpu.make_async_copy(
                source.at[:, pl.ds(z * LANES, LANES)], into.at[pl.ds(z * half_rows, half_rows)], sem.at[z]
            )
            for z in range(2)
        ]

    copies = [load(potential_hbm, potential, sems.at[4])]
    copies += [load(orbs_hbm.at[k], orbs.at[k], sems.at[k]) for k in range(4)]
    for pair in copies:
        for copy in pair:
            copy.start()

    def arrived(pair):
        for copy in pair:
            copy.wait()

    def place(entry):
        at = block[entry]
        return (at & 1) * half_rows + lax.shift_right_logical(at, 1)

    arrived(copies[0])

    def first(entry, carry):
        rows[4, pl.ds(entry, 1), :] = potential[pl.ds(place(entry), 1), :]
        counts[pl.ds(entry, 1), :] = jnp.full((1, LANES), count[entry], jnp.int32)
        return carry

    lax.fori_loop(0, ENTRIES, first, 0, unroll=8)
    for k in range(4):
        arrived(copies[k + 1])

        def step(entry, carry):
            rows[k, pl.ds(entry, 1), :] = orbs[k, pl.ds(place(entry), 1), :]
            return carry

        lax.fori_loop(0, ENTRIES, step, 0, unroll=8)

    piece = 64

    def reduce(index, carry):
        at = pl.ds(pl.multiple_of(index * piece, piece), piece)
        lane = lax.broadcasted_iota(jnp.int32, (piece, LANES), 1)
        cosine, sine = cos_sin((0.5 * TIME_STEP) * rows[4, at, :])
        inside = lane < counts[at, :]
        fields = []
        for n in range(ORBS):
            real, imag = rows[n, at, :], rows[ORBS + n, at, :]
            fields += [(n, cosine * real + sine * imag), (ORBS + n, cosine * imag - sine * real)]
        out = jnp.zeros((piece, LANES), jnp.float32)
        for f in range(4):
            masked = jnp.where(inside, projectors[f, at, :], 0.0)
            if f == 0:
                masked_ref[at, :] = masked
            for k, field in fields:
                total = jnp.sum(masked * field, axis=1, keepdims=True)
                out = jnp.where(lane == f * 4 + k, total, out)
        table[at, :] = out
        return carry

    lax.fori_loop(0, ENTRIES // piece, reduce, 0)
    turned = jnp.transpose(table[...])[:16]
    sums = lax.dot_general(
        three_parts(turned), atom_matrix(atom_ref), (((1,), (1,)), ((), ())), preferred_element_type=jnp.float32
    )
    sums = sums[:16] + sums[16:32] + sums[32:]
    for k in range(4):
        for q in range(4):
            packed[k * 4 + q : k * 4 + q + 1, :] = sums[k : k + 1, q * LANES : (q + 1) * LANES]
    slots = lax.dot_general(
        three_parts(sums), atom_matrix(slot_ref), (((1,), (1,)), ((), ())), preferred_element_type=jnp.float32
    )
    slots = slots[:16] + slots[16:32] + slots[32:]
    lane = lax.broadcasted_iota(jnp.int32, (8, LANES), 1)
    for d in range(GROUPS):
        tile = slots[:, d // 8 * LANES : (d // 8 + 1) * LANES]
        begin = d % 8 * OWNED
        upper = pltpu.roll(tile[:8], (LANES - begin) % LANES, 1)
        lower = pltpu.roll(tile[8:], (LANES - begin + OWNED) % LANES, 1)
        sent[d, 0:16, :] = packed[...]
        sent[d, 16:24, :] = jnp.where(lane < OWNED, upper, lower)


def project(orbs, potential, projectors, entry_atom, entry_block, entry_count, owner_slot):
    smem = pl.BlockSpec(memory_space=pltpu.SMEM)
    vmem = pl.BlockSpec(memory_space=pltpu.VMEM)
    hbm = pl.BlockSpec(memory_space=pltpu.HBM)
    rows = PLANES * SIZE
    return pl.pallas_call(
        project_kernel,
        out_shape=(
            jax.ShapeDtypeStruct((GROUPS, SENT, LANES), jnp.float32),
            jax.ShapeDtypeStruct((ENTRIES, LANES), jnp.float32),
        ),
        in_specs=[smem, smem, vmem, vmem, hbm, hbm, vmem],
        out_specs=(vmem, vmem),
        scratch_shapes=[
            pltpu.VMEM((4, 2 * rows, LANES), jnp.float32),
            pltpu.VMEM((2 * rows, LANES), jnp.float32),
            pltpu.VMEM((5, ENTRIES, LANES), jnp.float32),
            pltpu.VMEM((ENTRIES, LANES), jnp.int32),
            pltpu.VMEM((ENTRIES, LANES), jnp.float32),
            pltpu.VMEM((16, LANES), jnp.float32),
            pltpu.SemaphoreType.DMA((5, 2)),
        ],
        compiler_params=pltpu.CompilerParams(vmem_limit_bytes=VMEM),
        cost_estimate=pl.CostEstimate(flops=10**9, bytes_accessed=36 * 10**6, transcendentals=0),
        name="project",
    )(
        entry_block, entry_count, entry_atom.reshape(1, ENTRIES), owner_slot.reshape(1, ATOMS), orbs, potential, projectors
    )


SHIFT_STEP = 4


def shift_kernel(orbs, potential, *rest):
    out = rest[-1]
    for x in range(PLANES):
        cosine, sine = cos_sin((0.5 * TIME_STEP) * potential[x])
        real, imag = orbs[0, 0, x], orbs[1, 0, x]
        both = (cosine * real + sine * imag, cosine * imag - sine * real)
        for c in range(2):
            for d in range(SHIFT_STEP):
                for z in range(2):
                    tile = both[c][d * 8 : d * 8 + 8, z * LANES : (z + 1) * LANES]
                    out[d, pl.ds(c * 128 + z * 64 + x, 8, stride=8), :] = tile


def shift(n, orbitals, potential, *first):
    width = SHIFT_STEP * 8
    return pl.pallas_call(
        shift_kernel,
        grid=(GROUPS // SHIFT_STEP,),
        out_shape=jax.ShapeDtypeStruct((GROUPS, 256, LANES), jnp.float32),
        in_specs=[
            pl.BlockSpec((2, 1, PLANES, width, SIZE), lambda i: (0, n, 0, i, 0)),
            pl.BlockSpec((PLANES, width, SIZE), lambda i: (0, i, 0)),
            *[pl.BlockSpec(memory_space=pl.ANY) for _ in first],
        ],
        out_specs=pl.BlockSpec((SHIFT_STEP, 256, LANES), lambda i: (i, 0, 0)),
        compiler_params=pltpu.CompilerParams(vmem_limit_bytes=VMEM),
        cost_estimate=pl.CostEstimate(flops=10**8, bytes_accessed=11 * 10**6, transcendentals=0),
        name=f"shift{n}",
    )(orbitals, potential, *first)


def correct_kernel(n, place, received, strength, atom_ref, masked, before, after, field, coefs, updates, sems):
    load = pltpu.make_async_copy(before, field, sems.at[0])
    load.start()
    sums = jnp.sum(received[:, 0:16, :], axis=0)
    real = sums[n * 4 : n * 4 + 4]
    imag = sums[(ORBS + n) * 4 : (ORBS + n) * 4 + 4]
    cosine, sine = cos_sin(TIME_STEP * strength[...])
    less_one = cosine - 1.0
    both = (less_one * real + sine * imag, less_one * imag - sine * real)
    coefs[...] = jnp.zeros_like(coefs)
    for c in range(2):
        for q in range(4):
            coefs[c : c + 1, q * LANES : (q + 1) * LANES] = both[c][q : q + 1]
    spread = dot(three_parts(coefs[...]), atom_matrix(atom_ref))
    spread = jnp.transpose(spread[:16] + spread[16:32] + spread[32:])
    for c in range(2):
        updates[c] = spread[:, c : c + 1] * masked[...]
    load.wait()

    def step(entry, carry):
        row = place[entry]
        for c in range(2):
            at = pl.ds(row + c * 128, 1)
            field[at, :] = field[at, :] + updates[c, pl.ds(entry, 1), :]
        return carry

    lax.fori_loop(0, ENTRIES, step, 0, unroll=8)
    store = pltpu.make_async_copy(field, after, sems.at[1])
    store.start()
    store.wait()


def correct(n, place, received, strength, atoms, masked, before):
    smem = pl.BlockSpec(memory_space=pltpu.SMEM)
    vmem = pl.BlockSpec(memory_space=pltpu.VMEM)
    hbm = pl.BlockSpec(memory_space=pltpu.HBM)
    return pl.pallas_call(
        functools.partial(correct_kernel, n),
        out_shape=jax.ShapeDtypeStruct((GROUPS * 256, LANES), jnp.float32),
        in_specs=[smem, vmem, vmem, vmem, vmem, hbm],
        out_specs=hbm,
        scratch_shapes=[
            pltpu.VMEM((GROUPS * 256, LANES), jnp.float32),
            pltpu.VMEM((16, ATOMS), jnp.float32),
            pltpu.VMEM((2, ENTRIES, LANES), jnp.float32),
            pltpu.SemaphoreType.DMA((2,)),
        ],
        input_output_aliases={5: 0},
        compiler_params=pltpu.CompilerParams(vmem_limit_bytes=VMEM),
        cost_estimate=pl.CostEstimate(flops=5 * 10**8, bytes_accessed=20 * 10**6, transcendentals=0),
        name=f"correct{n}",
    )(place, received, strength, atoms, masked, before.reshape(GROUPS * 256, LANES))


def lines_kernel(n, field, left, right, *rest):
    *chunks, turned, sems = rest[-2 - len(CHUNKS) :]
    y = pl.program_id(0)
    real = [field[:, 0, z, 0].reshape(SIZE, LANES) for z in range(2)]
    imag = [field[:, 1, z, 0].reshape(SIZE, LANES) for z in range(2)]
    real, imag = propagate_lanes(right, real, imag)
    both = propagate_rows(left, real, imag)
    for c in range(2):
        for z in range(2):
            for d in range(GROUPS):
                tile = both[c][d * 8 : d * 8 + 8, z * LANES : (z + 1) * LANES]
                turned[d, c, z, pl.ds(y, 8, stride=8), :] = tile

    @pl.when(y == pl.num_programs(0) - 1)
    def _():
        copies, begin = [], 0
        for k, (chunk, planes) in enumerate(zip(chunks, CHUNKS)):
            part = turned.at[:, :, :, pl.ds(begin * 8, planes * 8)]
            copies.append(pltpu.make_async_copy(part, chunk.at[:, :, n], sems.at[k]))
            begin += planes
        for copy in copies:
            copy.start()
        for copy in copies:
            copy.wait()


def lines(n, field, left, right, before=(), first=()):
    hbm = pl.BlockSpec(memory_space=pltpu.HBM)
    return pl.pallas_call(
        functools.partial(lines_kernel, n),
        grid=(8,),
        out_shape=tuple(
            jax.ShapeDtypeStruct((GROUPS, 2, ORBS, 2, planes * 8, LANES), jnp.float32) for planes in CHUNKS
        ),
        in_specs=[
            pl.BlockSpec((GROUPS, 2, 2, 1, 8, LANES), lambda i: (0, 0, 0, i, 0, 0)),
            pl.BlockSpec(left.shape, lambda i: (0, 0, 0)),
            pl.BlockSpec(right.shape, lambda i: (0, 0, 0)),
            *[hbm for _ in (*before, *first)],
        ],
        out_specs=tuple(hbm for _ in CHUNKS),
        scratch_shapes=[
            pltpu.VMEM((GROUPS, 2, 2, 64, LANES), jnp.float32),
            pltpu.SemaphoreType.DMA((len(CHUNKS),)),
        ],
        input_output_aliases={3 + k: k for k in range(len(before))},
        compiler_params=pltpu.CompilerParams(vmem_limit_bytes=VMEM),
        cost_estimate=pl.CostEstimate(flops=5 * 10**9, bytes_accessed=10 * 10**6, transcendentals=0),
        name=f"lines{n}",
    )(field.reshape(GROUPS, 2, 2, 8, 8, LANES), left, right, *before, *first)


def finish_kernel(band, field, potential, left, *rest):
    out, *pieces, whole = rest[-6:]
    cosine, sine = cos_sin((0.5 * TIME_STEP) * potential[0])
    total = None
    for n in range(ORBS):
        real, imag = (
            jnp.concatenate([field[:, c, n, z].reshape(SIZE, LANES) for z in range(2)], axis=1) for c in range(2)
        )
        real, imag = propagate_rows(left, real, imag)
        real, imag = cosine * real + sine * imag, cosine * imag - sine * real
        out[0, n, 0] = real
        out[1, n, 0] = imag
        square = real * real + imag * imag
        total = square if total is None else total + square
    whole[...] = total
    rows = SIZE // BANDS
    for k, piece in enumerate(pieces):
        begin = pl.multiple_of((band[0] + k) % BANDS * rows, rows)
        piece[0] = whole[pl.ds(begin, rows), :]


def finish(planes, begin, band, field, potential, left, before=(), first=()):
    rows = SIZE // BANDS
    return pl.pallas_call(
        finish_kernel,
        grid=(planes,),
        out_shape=(
            jax.ShapeDtypeStruct((2, ORBS, PLANES, SIZE, SIZE), jnp.float32),
            *[jax.ShapeDtypeStruct((planes, rows, SIZE), jnp.float32) for _ in range(BANDS)],
        ),
        in_specs=[
            pl.BlockSpec(memory_space=pltpu.SMEM),
            pl.BlockSpec((GROUPS, 2, ORBS, 2, 8, LANES), lambda i: (0, 0, 0, 0, i, 0)),
            pl.BlockSpec((1, SIZE, SIZE), lambda i: (i + begin, 0, 0)),
            pl.BlockSpec(left.shape, lambda i: (0, 0, 0)),
            *[pl.BlockSpec(memory_space=pl.ANY) for _ in (*before, *first)],
        ],
        out_specs=(
            pl.BlockSpec((2, ORBS, 1, SIZE, SIZE), lambda i: (0, 0, i + begin, 0, 0)),
            *[pl.BlockSpec((1, rows, SIZE), lambda i: (i, 0, 0)) for _ in range(BANDS)],
        ),
        scratch_shapes=[pltpu.VMEM((SIZE, SIZE), jnp.float32)],
        input_output_aliases={4 + k: k for k in range(len(before))},
        compiler_params=pltpu.CompilerParams(vmem_limit_bytes=VMEM),
        cost_estimate=pl.CostEstimate(flops=10**9 * planes, bytes_accessed=3 * 10**6 * planes, transcendentals=0),
        name=f"finish{begin}",
    )(band, field, potential, left, *before, *first)


def collect_kernel(owners, band, *refs):
    out = refs[-1]
    rows = SIZE // BANDS
    for piece, (owner, offset) in zip(refs, owners):
        row = pl.multiple_of((band[0] + owner) % BANDS * rows, rows)
        out[0, pl.ds(pl.multiple_of(row + offset, rows // 2), piece.shape[1]), :] = piece[0]


def collect(begin, band, pieces, owners, *before):
    return pl.pallas_call(
        functools.partial(collect_kernel, owners),
        grid=(pieces[0].shape[0],),
        out_shape=jax.ShapeDtypeStruct((PLANES, SIZE, SIZE), jnp.float32),
        in_specs=[
            pl.BlockSpec(memory_space=pltpu.SMEM),
            *[pl.BlockSpec((1, piece.shape[1], SIZE), lambda i: (i, 0, 0)) for piece in pieces],
            *[pl.BlockSpec(memory_space=pl.ANY) for _ in before],
        ],
        out_specs=pl.BlockSpec((1, SIZE, SIZE), lambda i: (i + begin, 0, 0)),
        input_output_aliases={1 + len(pieces) + k: k for k in range(len(before))},
        compiler_params=pltpu.CompilerParams(vmem_limit_bytes=16 << 20),
        cost_estimate=pl.CostEstimate(flops=0, bytes_accessed=3 * 10**6, transcendentals=0),
        name=f"collect{begin}",
    )(band, *pieces, *before)


def onward(array, steps):
    return lax.ppermute(array, "band", [(b, (b + steps) % BANDS) for b in range(BANDS)])


def ring_reduce(pieces):
    own, right, across, left = pieces
    low, high = (slice(None), slice(0, SIZE // BANDS // 2)), (slice(None), slice(SIZE // BANDS // 2, None))
    right = right.at[low].add(onward(across[low], 1))
    left = left.at[high].add(onward(across[high], 3))
    return own + onward(right, 1) + onward(left, 3)


def ring_gather(total):
    before, after = onward(total, 1), onward(total, 3)
    half = SIZE // BANDS // 2
    pieces = total, before, after, onward(before[:, :half], 1), onward(after[:, half:], 3)
    return pieces, ((0, 0), (3, 0), (1, 0), (2, 0), (2, half))


def direct_reduce(pieces):
    return pieces[0] + onward(pieces[1], 1) + onward(pieces[2], 2) + onward(pieces[3], 3)


def direct_gather(total):
    return (total, *[onward(total, k) for k in range(1, BANDS)]), ((0, 0), (3, 0), (2, 0), (1, 0))


def exchange(array):
    return lax.all_to_all(array, "grid", split_axis=0, concat_axis=0, tiled=True)


def body(left, right, orbitals, potential, projectors, entry_atom, entry_block, entry_count, owner_slot, strength):
    atom_ids = jnp.arange(ATOMS, dtype=jnp.int32)
    rows = PLANES * SIZE
    band = lax.axis_index("band").astype(jnp.int32).reshape(1)
    sent, masked = project(
        orbitals.reshape(2 * ORBS, rows, SIZE), potential.reshape(rows, SIZE), projectors,
        entry_atom, entry_block, entry_count, owner_slot,
    )
    received = exchange(sent)
    x, y, z = entry_block // 512, (entry_block // 2) % SIZE, entry_block % 2
    place = (y // 8) * 256 + z * 64 + (y % 8) * 8 + x
    in_slot = owner_slot[:, None] == atom_ids[None, :]
    strength_atom = jnp.sum(jnp.where(in_slot, strength[None, :], 0.0), axis=1).reshape(4, LANES)
    atoms = entry_atom.reshape(1, ENTRIES)
    pencils, sent = [], ()
    for n in range(ORBS):
        shifted = shift(n, orbitals, potential, *sent)
        fixed = correct(n, place, received, strength_atom, atoms, masked, shifted)
        pencils.append(exchange(fixed.reshape(GROUPS, 256, LANES)))
        sent = (fixed,)
    mine = jnp.sum(received[:, 16:], axis=0)
    mine = jnp.concatenate([mine[:, :OWNED], mine[:, OWNED : 2 * OWNED]], axis=0).reshape(4, 2 * ORBS, OWNED)
    strength_mine = lax.dynamic_slice_in_dim(strength, lax.axis_index("grid") * OWNED, OWNED)
    forces = -2.0 * strength_mine * jnp.sum(mine[0][None] * mine[1:], axis=1)
    forces = sum([onward(forces, k) for k in range(1, BANDS)], forces)

    back = lines(0, pencils[0], left, right)
    back = lines(1, pencils[1], left, right, back, (forces,))
    out, density, ready, begin = (), (), (), 0
    for k, planes in enumerate(CHUNKS):
        field = exchange(back[k])
        made, *pieces = finish(planes, begin, band, field, potential, left, out, ready)
        out = (made,)
        if k == 0:
            density = (collect(begin, band, *ring_gather(ring_reduce(pieces))),)
            ready = density
        else:
            total = direct_reduce(pieces)
            ready = (total,)
            density = (collect(begin, band, *direct_gather(total), *density),)
        begin += planes
    return out[0], density[0], forces


def solution(mesh):
    left, right = propagator_tables()
    in_specs = (
        P(None, "band", "grid", None, None),
        P("grid", None, None),
        P(None, "grid", None),
        P("grid"),
        P("grid"),
        P("grid"),
        P(),
        P(),
    )
    out_specs = (P(None, "band", "grid", None, None), P("grid", None, None), P(None, "grid"))

    def run(*args):
        return body(jnp.asarray(left), jnp.asarray(right), *args)

    return jax.shard_map(run, mesh=mesh, in_specs=in_specs, out_specs=out_specs, check_vma=False)
```

```python
import functools
import math

import jax
import jax.numpy as jnp
import ml_dtypes
import numpy as np
from jax import lax
from jax.experimental import pallas as pl
from jax.experimental.pallas import tpu as pltpu
from jax.sharding import PartitionSpec as P

SIZE = 256
HALF = SIZE // 2
LANES = 128
TIME_STEP = 4.0
HIGHEST = lax.Precision.HIGHEST
ORBS = 2
BANDS = 4
PLANES = 8
GROUPS = 32
ENTRIES = 512
ATOMS = 512
OWNED = ATOMS // GROUPS
CHUNKS = (5, 3)
VMEM = 56 << 20
SENT = 24


def propagator_tables():
    index = np.arange(SIZE)
    freq = np.where(index < HALF, index, index - SIZE)
    wave = freq * (2.0 * math.pi / SIZE)
    line = np.fft.ifft(np.exp(-0.5j * TIME_STEP * wave * wave))
    full = line[(index[:, None] - index[None, :]) % SIZE]
    left = []
    for sign in (1.0, -1.0):
        half = 0.5 * (full[:HALF, :HALF] + sign * full[:HALF, HALF:])
        real = np.block([[half.real, -half.imag], [half.imag, half.real]]).astype(np.float32)
        high = real.astype(ml_dtypes.bfloat16)
        low = (real - high.astype(np.float32)).astype(ml_dtypes.bfloat16)
        left.append(np.concatenate([high, high, low], axis=1))
    left = np.stack(left)
    return left, np.ascontiguousarray(np.swapaxes(left, 1, 2))


def cos_sin(angle):
    turns = jnp.floor(angle * (2.0 / math.pi) + 0.5)
    rest = angle - turns * 1.5703125
    rest = rest - turns * 4.837512969970703125e-4
    rest = rest - turns * 7.54978995489188216e-8
    square = rest * rest
    sine = ((-1.9515295891e-4 * square + 8.3321608736e-3) * square - 1.6666654611e-1) * square * rest + rest
    cosine = ((2.443315711809948e-5 * square - 1.388731625493765e-3) * square + 4.166664568298827e-2) * (
        square * square
    ) - 0.5 * square + 1.0
    quarter = turns.astype(jnp.int32)
    odd = (quarter & 1) == 1
    cos_out = jnp.where(odd, sine, cosine)
    sin_out = jnp.where(odd, cosine, sine)
    cos_out = jnp.where(((quarter + 1) & 2) == 2, -cos_out, cos_out)
    sin_out = jnp.where((quarter & 2) == 2, -sin_out, sin_out)
    return cos_out, sin_out


def split(values, axis):
    high = values.astype(jnp.bfloat16)
    low = (values - high.astype(jnp.float32)).astype(jnp.bfloat16)
    return jnp.concatenate([high, low, high], axis=axis)


def three_parts(values):
    high = values.astype(jnp.bfloat16)
    rest = values - high.astype(jnp.float32)
    middle = rest.astype(jnp.bfloat16)
    low = (rest - middle.astype(jnp.float32)).astype(jnp.bfloat16)
    return jnp.concatenate([high, middle, low], axis=0)


def dot(left, right):
    return jnp.dot(left, right, preferred_element_type=jnp.float32)


def propagate_rows(table, real, imag):
    plus = jnp.concatenate([real[:HALF] + real[HALF:], imag[:HALF] + imag[HALF:]], axis=0)
    minus = jnp.concatenate([real[:HALF] - real[HALF:], imag[:HALF] - imag[HALF:]], axis=0)
    plus = dot(table[0], split(plus, 0))
    minus = dot(table[1], split(minus, 0))
    low, high = plus + minus, plus - minus
    return (
        jnp.concatenate([low[:HALF], high[:HALF]], axis=0),
        jnp.concatenate([low[HALF:], high[HALF:]], axis=0),
    )


def propagate_lanes(table, real, imag):
    plus = jnp.concatenate([real[0] + real[1], imag[0] + imag[1]], axis=1)
    minus = jnp.concatenate([real[0] - real[1], imag[0] - imag[1]], axis=1)
    plus = dot(split(plus, 1), table[0])
    minus = dot(split(minus, 1), table[1])
    low, high = plus + minus, plus - minus
    return (
        jnp.concatenate([low[:, :HALF], high[:, :HALF]], axis=1),
        jnp.concatenate([low[:, HALF:], high[:, HALF:]], axis=1),
    )


def atom_matrix(atom_ref):
    atoms = lax.broadcasted_iota(jnp.int32, (ATOMS, ENTRIES), 0)
    return jnp.where(atoms == atom_ref[...], 1.0, 0.0).astype(jnp.bfloat16)


def project_kernel(
    block, count, atom_ref, slot_ref, orbs_hbm, potential_hbm, projectors_hbm, sent, masked_ref,
    orbs, potential, projectors, rows, counts, table, packed, sems,
):
    half_rows = PLANES * SIZE

    def load(source, into, sem):
        return [
            pltpu.make_async_copy(
                source.at[:, pl.ds(z * LANES, LANES)], into.at[pl.ds(z * half_rows, half_rows)], sem.at[z]
            )
            for z in range(2)
        ]

    copies = [load(potential_hbm, potential, sems.at[4])]
    copies += [load(orbs_hbm.at[k], orbs.at[k], sems.at[k]) for k in range(4)]
    projectors_copy = pltpu.make_async_copy(projectors_hbm, projectors, sems.at[5, 0])
    for pair in copies:
        for copy in pair:
            copy.start()
    projectors_copy.start()

    def arrived(pair):
        for copy in pair:
            copy.wait()

    def place(entry):
        at = block[entry]
        return (at & 1) * half_rows + lax.shift_right_logical(at, 1)

    arrived(copies[0])

    def first(entry, carry):
        rows[4, pl.ds(entry, 1), :] = potential[pl.ds(place(entry), 1), :]
        counts[pl.ds(entry, 1), :] = jnp.full((1, LANES), count[entry], jnp.int32)
        return carry

    lax.fori_loop(0, ENTRIES, first, 0, unroll=8)
    cosine, sine = cos_sin((0.5 * TIME_STEP) * rows[4])
    rows[4] = cosine
    rows[5] = sine
    for k in range(4):
        arrived(copies[k + 1])

        def step(entry, carry):
            rows[k, pl.ds(entry, 1), :] = orbs[k, pl.ds(place(entry), 1), :]
            return carry

        lax.fori_loop(0, ENTRIES, step, 0, unroll=8)

    projectors_copy.wait()
    piece = 64

    def reduce(index, carry):
        at = pl.ds(pl.multiple_of(index * piece, piece), piece)
        lane = lax.broadcasted_iota(jnp.int32, (piece, LANES), 1)
        cosine, sine = rows[4, at, :], rows[5, at, :]
        inside = lane < counts[at, :]
        fields = []
        for n in range(ORBS):
            real, imag = rows[n, at, :], rows[ORBS + n, at, :]
            fields += [(n, cosine * real + sine * imag), (ORBS + n, cosine * imag - sine * real)]
        out = jnp.zeros((piece, LANES), jnp.float32)
        for f in range(4):
            masked = jnp.where(inside, projectors[f, at, :], 0.0)
            if f == 0:
                masked_ref[at, :] = masked
            for k, field in fields:
                total = jnp.sum(masked * field, axis=1, keepdims=True)
                out = jnp.where(lane == f * 4 + k, total, out)
        table[at, :] = out
        return carry

    lax.fori_loop(0, ENTRIES // piece, reduce, 0)
    turned = jnp.transpose(table[...])[:16]
    sums = lax.dot_general(
        three_parts(turned), atom_matrix(atom_ref), (((1,), (1,)), ((), ())), preferred_element_type=jnp.float32
    )
    sums = sums[:16] + sums[16:32] + sums[32:]
    for k in range(4):
        for q in range(4):
            packed[k * 4 + q : k * 4 + q + 1, :] = sums[k : k + 1, q * LANES : (q + 1) * LANES]
    slots = lax.dot_general(
        three_parts(sums), atom_matrix(slot_ref), (((1,), (1,)), ((), ())), preferred_element_type=jnp.float32
    )
    slots = slots[:16] + slots[16:32] + slots[32:]
    lane = lax.broadcasted_iota(jnp.int32, (8, LANES), 1)
    for d in range(GROUPS):
        tile = slots[:, d // 8 * LANES : (d // 8 + 1) * LANES]
        begin = d % 8 * OWNED
        upper = pltpu.roll(tile[:8], (LANES - begin) % LANES, 1)
        lower = pltpu.roll(tile[8:], (LANES - begin + OWNED) % LANES, 1)
        sent[d, 0:16, :] = packed[...]
        sent[d, 16:24, :] = jnp.where(lane < OWNED, upper, lower)


def project(orbs, potential, projectors, entry_atom, entry_block, entry_count, owner_slot):
    smem = pl.BlockSpec(memory_space=pltpu.SMEM)
    vmem = pl.BlockSpec(memory_space=pltpu.VMEM)
    hbm = pl.BlockSpec(memory_space=pltpu.HBM)
    rows = PLANES * SIZE
    return pl.pallas_call(
        project_kernel,
        out_shape=(
            jax.ShapeDtypeStruct((GROUPS, SENT, LANES), jnp.float32),
            jax.ShapeDtypeStruct((ENTRIES, LANES), jnp.float32),
        ),
        in_specs=[smem, smem, vmem, vmem, hbm, hbm, hbm],
        out_specs=(vmem, vmem),
        scratch_shapes=[
            pltpu.VMEM((4, 2 * rows, LANES), jnp.float32),
            pltpu.VMEM((2 * rows, LANES), jnp.float32),
            pltpu.VMEM((4, ENTRIES, LANES), jnp.float32),
            pltpu.VMEM((6, ENTRIES, LANES), jnp.float32),
            pltpu.VMEM((ENTRIES, LANES), jnp.int32),
            pltpu.VMEM((ENTRIES, LANES), jnp.float32),
            pltpu.VMEM((16, LANES), jnp.float32),
            pltpu.SemaphoreType.DMA((6, 2)),
        ],
        compiler_params=pltpu.CompilerParams(vmem_limit_bytes=VMEM),
        cost_estimate=pl.CostEstimate(flops=10**9, bytes_accessed=36 * 10**6, transcendentals=0),
        name="project",
    )(
        entry_block, entry_count, entry_atom.reshape(1, ENTRIES), owner_slot.reshape(1, ATOMS), orbs, potential, projectors
    )


SHIFT_STEP = 8


def shift_kernel(orbs, potential, *rest):
    out = rest[-1]
    for x in range(PLANES):
        cosine, sine = cos_sin((0.5 * TIME_STEP) * potential[x])
        real, imag = orbs[0, 0, x], orbs[1, 0, x]
        both = (cosine * real + sine * imag, cosine * imag - sine * real)
        for c in range(2):
            for d in range(SHIFT_STEP):
                for z in range(2):
                    tile = both[c][d * 8 : d * 8 + 8, z * LANES : (z + 1) * LANES]
                    out[pl.ds(d * 256 + c * 16 + z * 8 + x, 8, stride=32), :] = tile


def shift(n, orbitals, potential, *first):
    width = SHIFT_STEP * 8
    return pl.pallas_call(
        shift_kernel,
        grid=(GROUPS // SHIFT_STEP,),
        out_shape=pltpu.HBM((GROUPS * 256, LANES), jnp.float32),
        in_specs=[
            pl.BlockSpec((2, 1, PLANES, width, SIZE), lambda i: (0, n, 0, i, 0)),
            pl.BlockSpec((PLANES, width, SIZE), lambda i: (0, i, 0)),
            *[pl.BlockSpec(memory_space=pl.ANY) for _ in first],
        ],
        out_specs=pl.BlockSpec((SHIFT_STEP * 256, LANES), lambda i: (i, 0)),
        compiler_params=pltpu.CompilerParams(vmem_limit_bytes=VMEM),
        cost_estimate=pl.CostEstimate(flops=10**8, bytes_accessed=11 * 10**6, transcendentals=0),
        name=f"shift{n}",
    )(orbitals, potential, *first)


def correct_kernel(n, place, received, strength, atom_ref, masked, before, after, field, coefs, updates, sems):
    load = pltpu.make_async_copy(before, field, sems.at[0])
    load.start()
    sums = jnp.sum(received[:, 0:16, :], axis=0)
    real = sums[n * 4 : n * 4 + 4]
    imag = sums[(ORBS + n) * 4 : (ORBS + n) * 4 + 4]
    cosine, sine = cos_sin(TIME_STEP * strength[...])
    less_one = cosine - 1.0
    both = (less_one * real + sine * imag, less_one * imag - sine * real)
    coefs[...] = jnp.zeros_like(coefs)
    for c in range(2):
        for q in range(4):
            coefs[c : c + 1, q * LANES : (q + 1) * LANES] = both[c][q : q + 1]
    spread = dot(three_parts(coefs[...]), atom_matrix(atom_ref))
    spread = jnp.transpose(spread[:16] + spread[16:32] + spread[32:])
    for c in range(2):
        updates[c] = spread[:, c : c + 1] * masked[...]
    load.wait()

    def step(entry, carry):
        row = place[entry]
        at = [pl.ds(row + c * 16, 1) for c in range(2)]
        both = [field[at[c], :] + updates[c, pl.ds(entry, 1), :] for c in range(2)]
        for c in range(2):
            field[at[c], :] = both[c]
        return carry

    lax.fori_loop(0, ENTRIES, step, 0, unroll=8)
    store = pltpu.make_async_copy(field, after, sems.at[1])
    store.start()
    store.wait()


def correct(n, place, received, strength, atoms, masked, before):
    smem = pl.BlockSpec(memory_space=pltpu.SMEM)
    vmem = pl.BlockSpec(memory_space=pltpu.VMEM)
    hbm = pl.BlockSpec(memory_space=pltpu.HBM)
    return pl.pallas_call(
        functools.partial(correct_kernel, n),
        out_shape=pltpu.HBM((GROUPS * 256, LANES), jnp.float32),
        in_specs=[smem, vmem, vmem, vmem, vmem, hbm],
        out_specs=hbm,
        scratch_shapes=[
            pltpu.VMEM((GROUPS * 256, LANES), jnp.float32),
            pltpu.VMEM((16, ATOMS), jnp.float32),
            pltpu.VMEM((2, ENTRIES, LANES), jnp.float32),
            pltpu.SemaphoreType.DMA((2,)),
        ],
        input_output_aliases={5: 0},
        compiler_params=pltpu.CompilerParams(vmem_limit_bytes=24 << 20),
        cost_estimate=pl.CostEstimate(flops=5 * 10**8, bytes_accessed=20 * 10**6, transcendentals=0),
        name=f"correct{n}",
    )(place, received, strength, atoms, masked, before)


LINES_STEP = 4


def lines_kernel(n, field, left, right, *rest):
    *chunks, half_done, turned, sems = rest[-3 - len(CHUNKS) :]
    step = pl.program_id(0)
    for k in range(LINES_STEP):
        real, imag = ([field[:, k, c, z].reshape(SIZE, LANES) for z in range(2)] for c in range(2))
        both = propagate_lanes(right, real, imag)
        y = step * LINES_STEP + k
        for c in range(2):
            for z in range(2):
                half_done[c, z, y] = both[c][:, z * LANES : (z + 1) * LANES]

    @pl.when(step == pl.num_programs(0) - 1)
    def _():
        rows = turned.reshape(GROUPS, 2, PLANES * 16, LANES)
        copies = []
        for z in range(2):
            for y in range(0, 8, 2):
                real, imag = (
                    jnp.concatenate([half_done[c, z, y], half_done[c, z, y + 1]], axis=1) for c in range(2)
                )
                both = propagate_rows(left, real, imag)
                for c in range(2):
                    for k in range(2):
                        for d in range(GROUPS):
                            tile = both[c][d * 8 : d * 8 + 8, k * LANES : (k + 1) * LANES]
                            rows[d, z, pl.ds(c * 8 + y + k, 8, stride=16), :] = tile
            begin = 0
            for k, (chunk, planes) in enumerate(zip(chunks, CHUNKS)):
                part = turned.at[:, z, pl.ds(begin, planes)]
                copies.append(pltpu.make_async_copy(part, chunk.at[:, :, n, z], sems.at[z, k]))
                copies[-1].start()
                begin += planes
        for copy in copies:
            copy.wait()


def lines(n, field, left, right, before=(), first=()):
    hbm = pl.BlockSpec(memory_space=pltpu.HBM)
    return pl.pallas_call(
        functools.partial(lines_kernel, n),
        grid=(8 // LINES_STEP,),
        out_shape=tuple(
            jax.ShapeDtypeStruct((GROUPS, planes, ORBS, 2, 16, LANES), jnp.float32) for planes in CHUNKS
        ),
        in_specs=[
            pl.BlockSpec((GROUPS, LINES_STEP, 2, 2, 8, LANES), lambda i: (0, i, 0, 0, 0, 0)),
            pl.BlockSpec(left.shape, lambda i: (0, 0, 0)),
            pl.BlockSpec(right.shape, lambda i: (0, 0, 0)),
            *[hbm for _ in (*before, *first)],
        ],
        out_specs=tuple(hbm for _ in CHUNKS),
        scratch_shapes=[
            pltpu.VMEM((2, 2, 8, SIZE, LANES), jnp.float32),
            pltpu.VMEM((GROUPS, 2, PLANES, 16, LANES), jnp.float32),
            pltpu.SemaphoreType.DMA((2, len(CHUNKS))),
        ],
        input_output_aliases={3 + k: k for k in range(len(before))},
        compiler_params=pltpu.CompilerParams(vmem_limit_bytes=VMEM),
        cost_estimate=pl.CostEstimate(flops=5 * 10**9, bytes_accessed=10 * 10**6, transcendentals=0),
        name=f"lines{n}",
    )(field.reshape(GROUPS, 8, 2, 2, 8, LANES), left, right, *before, *first)


def finish_kernel(halves, band, field, potential, left, *rest):
    out, *pieces, whole = rest[-2 - BANDS * halves :]
    cosine, sine = cos_sin((0.5 * TIME_STEP) * potential[0])
    total = None
    for n in range(ORBS):
        real, imag = (
            jnp.concatenate([field[:, 0, n, z, c].reshape(SIZE, LANES) for z in range(2)], axis=1) for c in range(2)
        )
        real, imag = propagate_rows(left, real, imag)
        real, imag = cosine * real + sine * imag, cosine * imag - sine * real
        out[0, n, 0] = real
        out[1, n, 0] = imag
        square = real * real + imag * imag
        total = square if total is None else total + square
    whole[...] = total
    rows = SIZE // BANDS // halves
    for k, piece in enumerate(pieces):
        begin = (band[0] + k // halves) % BANDS * halves + k % halves
        piece[0] = whole[pl.ds(pl.multiple_of(begin * rows, rows), rows), :]


def finish(planes, begin, halves, band, field, potential, left, before=(), first=()):
    rows = SIZE // BANDS // halves
    return pl.pallas_call(
        functools.partial(finish_kernel, halves),
        grid=(planes,),
        out_shape=(
            jax.ShapeDtypeStruct((2, ORBS, PLANES, SIZE, SIZE), jnp.float32),
            *[jax.ShapeDtypeStruct((planes, rows, SIZE), jnp.float32) for _ in range(BANDS * halves)],
        ),
        in_specs=[
            pl.BlockSpec(memory_space=pltpu.SMEM),
            pl.BlockSpec((GROUPS, 1, ORBS, 2, 2, 8, LANES), lambda i: (0, i, 0, 0, 0, 0, 0)),
            pl.BlockSpec((1, SIZE, SIZE), lambda i: (i + begin, 0, 0)),
            pl.BlockSpec(left.shape, lambda i: (0, 0, 0)),
            *[pl.BlockSpec(memory_space=pl.ANY) for _ in (*before, *first)],
        ],
        out_specs=(
            pl.BlockSpec((2, ORBS, 1, SIZE, SIZE), lambda i: (0, 0, i + begin, 0, 0)),
            *[pl.BlockSpec((1, rows, SIZE), lambda i: (i, 0, 0)) for _ in range(BANDS * halves)],
        ),
        scratch_shapes=[pltpu.VMEM((SIZE, SIZE), jnp.float32)],
        input_output_aliases={4 + k: k for k in range(len(before))},
        compiler_params=pltpu.CompilerParams(vmem_limit_bytes=VMEM),
        cost_estimate=pl.CostEstimate(flops=10**9 * planes, bytes_accessed=3 * 10**6 * planes, transcendentals=0),
        name=f"finish{begin}",
    )(band, field.reshape(GROUPS, planes, ORBS, 2, 2, 8, LANES), potential, left, *before, *first)


def collect_kernel(owners, band, *refs):
    out = refs[-1]
    rows = SIZE // BANDS
    for piece, (owner, offset) in zip(refs, owners):
        row = pl.multiple_of((band[0] + owner) % BANDS * rows, rows)
        out[0, pl.ds(pl.multiple_of(row + offset, rows // 2), piece.shape[1]), :] = piece[0]


def collect(begin, band, pieces, owners, *before):
    return pl.pallas_call(
        functools.partial(collect_kernel, owners),
        grid=(pieces[0].shape[0],),
        out_shape=jax.ShapeDtypeStruct((PLANES, SIZE, SIZE), jnp.float32),
        in_specs=[
            pl.BlockSpec(memory_space=pltpu.SMEM),
            *[pl.BlockSpec((1, piece.shape[1], SIZE), lambda i: (i, 0, 0)) for piece in pieces],
            *[pl.BlockSpec(memory_space=pltpu.HBM) for _ in before],
        ],
        out_specs=pl.BlockSpec((1, SIZE, SIZE), lambda i: (i + begin, 0, 0)),
        input_output_aliases={1 + len(pieces) + k: k for k in range(len(before))},
        compiler_params=pltpu.CompilerParams(vmem_limit_bytes=VMEM),
        cost_estimate=pl.CostEstimate(flops=0, bytes_accessed=3 * 10**6, transcendentals=0),
        name=f"collect{begin}",
    )(band, *pieces, *before)


def onward(array, steps):
    return lax.ppermute(array, "band", [(b, (b + steps) % BANDS) for b in range(BANDS)])


def ring_reduce(pieces):
    own_low, own_high, next_low, next_high, across_low, across_high, last_low, last_high = pieces
    from_last = onward(across_low, 1)
    from_next = onward(across_high, 3)
    high = own_high + onward(next_high, 1)
    low = own_low + onward(last_low, 3)
    return low + onward(next_low + from_last, 1), high + onward(last_high + from_next, 3)


def ring_gather(low, high):
    last_low, next_high = onward(low, 1), onward(high, 3)
    last_high, next_low = onward(high, 1), onward(low, 3)
    pieces = low, high, last_low, last_high, next_low, next_high, onward(last_low, 1), onward(next_high, 3)
    half = SIZE // BANDS // 2
    return pieces, tuple((owner, offset) for owner in (0, 3, 1, 2) for offset in (0, half))


def add_kernel(own, from_last, across, from_next, *rest):
    rest[-1][...] = own[...] + from_last[...] + across[...] + from_next[...]


def direct_reduce(pieces, first):
    parts = [pieces[0], *[onward(pieces[k], k) for k in range(1, BANDS)]]
    return pl.pallas_call(
        add_kernel,
        out_shape=jax.ShapeDtypeStruct(pieces[0].shape, jnp.float32),
        in_specs=[
            *[pl.BlockSpec(memory_space=pltpu.VMEM) for _ in parts],
            *[pl.BlockSpec(memory_space=pltpu.HBM) for _ in first],
        ],
        out_specs=pl.BlockSpec(memory_space=pltpu.VMEM),
        compiler_params=pltpu.CompilerParams(vmem_limit_bytes=VMEM),
        cost_estimate=pl.CostEstimate(flops=10**6, bytes_accessed=10**6, transcendentals=0),
        name="add",
    )(*parts, *first)


def direct_gather(total):
    return (total, *[onward(total, k) for k in range(1, BANDS)]), ((0, 0), (3, 0), (2, 0), (1, 0))


def exchange(array):
    return lax.all_to_all(array, "grid", split_axis=0, concat_axis=0, tiled=True)


def body(left, right, orbitals, potential, projectors, entry_atom, entry_block, entry_count, owner_slot, strength):
    atom_ids = jnp.arange(ATOMS, dtype=jnp.int32)
    rows = PLANES * SIZE
    band = lax.axis_index("band").astype(jnp.int32).reshape(1)
    sent, masked = project(
        orbitals.reshape(2 * ORBS, rows, SIZE), potential.reshape(rows, SIZE), projectors,
        entry_atom, entry_block, entry_count, owner_slot,
    )
    received = exchange(sent)
    x, y, z = entry_block // 512, (entry_block // 2) % SIZE, entry_block % 2
    place = y * 32 + z * 8 + x
    in_slot = owner_slot[:, None] == atom_ids[None, :]
    strength_atom = jnp.sum(jnp.where(in_slot, strength[None, :], 0.0), axis=1).reshape(4, LANES)
    atoms = entry_atom.reshape(1, ENTRIES)
    pencils, sent = [], ()
    for n in range(ORBS):
        shifted = shift(n, orbitals, potential, *sent)
        fixed = correct(n, place, received, strength_atom, atoms, masked, shifted)
        pencils.append(exchange(fixed.reshape(GROUPS, 256, LANES)))
        sent = (fixed,)
    mine = jnp.sum(received[:, 16:], axis=0)
    mine = jnp.concatenate([mine[:, :OWNED], mine[:, OWNED : 2 * OWNED]], axis=0).reshape(4, 2 * ORBS, OWNED)
    strength_mine = lax.dynamic_slice_in_dim(strength, lax.axis_index("grid") * OWNED, OWNED)
    forces = -2.0 * strength_mine * jnp.sum(mine[0][None] * mine[1:], axis=1)
    forces = sum([onward(forces, k) for k in range(1, BANDS)], forces)

    back = lines(0, pencils[0], left, right)
    back = lines(1, pencils[1], left, right, back, (forces,))
    out, density, ready, begin = (), (), (), 0
    for k, planes in enumerate(CHUNKS):
        field = exchange(back[k])
        made, *pieces = finish(planes, begin, 2 if k == 0 else 1, band, field, potential, left, out, ready)
        out = (made,)
        if k == 0:
            sums, owners = ring_gather(*ring_reduce(pieces))
            ready = sums[2:]
        else:
            sums, owners = direct_gather(direct_reduce(pieces, density))
        density = (collect(begin, band, sums, owners, *density),)
        begin += planes
    return out[0], density[0], forces


def solution(mesh):
    left, right = propagator_tables()
    in_specs = (
        P(None, "band", "grid", None, None),
        P("grid", None, None),
        P(None, "grid", None),
        P("grid"),
        P("grid"),
        P("grid"),
        P(),
        P(),
    )
    out_specs = (P(None, "band", "grid", None, None), P("grid", None, None), P(None, "grid"))

    def run(*args):
        return body(jnp.asarray(left), jnp.asarray(right), *args)

    return jax.shard_map(run, mesh=mesh, in_specs=in_specs, out_specs=out_specs, check_vma=False)
```

```python
import functools
import math

import jax
import jax.numpy as jnp
import ml_dtypes
import numpy as np
from jax import lax
from jax.experimental import pallas as pl
from jax.experimental.pallas import tpu as pltpu
from jax.sharding import PartitionSpec as P

SIZE = 256
HALF = SIZE // 2
LANES = 128
TIME_STEP = 4.0
HIGHEST = lax.Precision.HIGHEST
ORBS = 2
BANDS = 4
PLANES = 8
GROUPS = 32
ENTRIES = 512
ATOMS = 512
OWNED = ATOMS // GROUPS
CHUNKS = (5, 3)
VMEM = 56 << 20
SENT = 24


def propagator_tables():
    index = np.arange(SIZE)
    freq = np.where(index < HALF, index, index - SIZE)
    wave = freq * (2.0 * math.pi / SIZE)
    line = np.fft.ifft(np.exp(-0.5j * TIME_STEP * wave * wave))
    full = line[(index[:, None] - index[None, :]) % SIZE]
    left = []
    for sign in (1.0, -1.0):
        half = 0.5 * (full[:HALF, :HALF] + sign * full[:HALF, HALF:])
        real = np.block([[half.real, -half.imag], [half.imag, half.real]]).astype(np.float32)
        high = real.astype(ml_dtypes.bfloat16)
        low = (real - high.astype(np.float32)).astype(ml_dtypes.bfloat16)
        left.append(np.concatenate([high, high, low], axis=1))
    left = np.stack(left)
    return left, np.ascontiguousarray(np.swapaxes(left, 1, 2))


def cos_sin(angle):
    turns = jnp.floor(angle * (2.0 / math.pi) + 0.5)
    rest = angle - turns * 1.5703125
    rest = rest - turns * 4.837512969970703125e-4
    rest = rest - turns * 7.54978995489188216e-8
    square = rest * rest
    sine = ((-1.9515295891e-4 * square + 8.3321608736e-3) * square - 1.6666654611e-1) * square * rest + rest
    cosine = ((2.443315711809948e-5 * square - 1.388731625493765e-3) * square + 4.166664568298827e-2) * (
        square * square
    ) - 0.5 * square + 1.0
    quarter = turns.astype(jnp.int32)
    odd = (quarter & 1) == 1
    cos_out = jnp.where(odd, sine, cosine)
    sin_out = jnp.where(odd, cosine, sine)
    cos_out = jnp.where(((quarter + 1) & 2) == 2, -cos_out, cos_out)
    sin_out = jnp.where((quarter & 2) == 2, -sin_out, sin_out)
    return cos_out, sin_out


def split(values, axis):
    high = values.astype(jnp.bfloat16)
    low = (values - high.astype(jnp.float32)).astype(jnp.bfloat16)
    return jnp.concatenate([high, low, high], axis=axis)


def three_parts(values):
    high = values.astype(jnp.bfloat16)
    rest = values - high.astype(jnp.float32)
    middle = rest.astype(jnp.bfloat16)
    low = (rest - middle.astype(jnp.float32)).astype(jnp.bfloat16)
    return jnp.concatenate([high, middle, low], axis=0)


def dot(left, right):
    return jnp.dot(left, right, preferred_element_type=jnp.float32)


def propagate_rows(table, real, imag):
    plus = jnp.concatenate([real[:HALF] + real[HALF:], imag[:HALF] + imag[HALF:]], axis=0)
    minus = jnp.concatenate([real[:HALF] - real[HALF:], imag[:HALF] - imag[HALF:]], axis=0)
    plus = dot(table[0], split(plus, 0))
    minus = dot(table[1], split(minus, 0))
    low, high = plus + minus, plus - minus
    return (
        jnp.concatenate([low[:HALF], high[:HALF]], axis=0),
        jnp.concatenate([low[HALF:], high[HALF:]], axis=0),
    )


def propagate_lanes(table, real, imag):
    plus = jnp.concatenate([real[0] + real[1], imag[0] + imag[1]], axis=1)
    minus = jnp.concatenate([real[0] - real[1], imag[0] - imag[1]], axis=1)
    plus = dot(split(plus, 1), table[0])
    minus = dot(split(minus, 1), table[1])
    low, high = plus + minus, plus - minus
    return (
        jnp.concatenate([low[:, :HALF], high[:, :HALF]], axis=1),
        jnp.concatenate([low[:, HALF:], high[:, HALF:]], axis=1),
    )


def atom_matrix(atom_ref):
    atoms = lax.broadcasted_iota(jnp.int32, (ATOMS, ENTRIES), 0)
    return jnp.where(atoms == atom_ref[...], 1.0, 0.0).astype(jnp.bfloat16)


def project_kernel(
    block, count, atom_ref, slot_ref, orbs_hbm, potential_hbm, projectors_hbm, sent, masked_ref,
    orbs, potential, projectors, rows, counts, table, packed, sems,
):
    half_rows = PLANES * SIZE

    def load(source, into, sem):
        return [
            pltpu.make_async_copy(
                source.at[:, pl.ds(z * LANES, LANES)], into.at[pl.ds(z * half_rows, half_rows)], sem.at[z]
            )
            for z in range(2)
        ]

    copies = [load(potential_hbm, potential, sems.at[4])]
    copies += [load(orbs_hbm.at[k], orbs.at[k], sems.at[k]) for k in range(4)]
    projectors_copy = pltpu.make_async_copy(projectors_hbm, projectors, sems.at[5, 0])
    for pair in copies:
        for copy in pair:
            copy.start()
    projectors_copy.start()

    def arrived(pair):
        for copy in pair:
            copy.wait()

    def place(entry):
        at = block[entry]
        return (at & 1) * half_rows + lax.shift_right_logical(at, 1)

    arrived(copies[0])

    def first(entry, carry):
        rows[4, pl.ds(entry, 1), :] = potential[pl.ds(place(entry), 1), :]
        counts[pl.ds(entry, 1), :] = jnp.full((1, LANES), count[entry], jnp.int32)
        return carry

    lax.fori_loop(0, ENTRIES, first, 0, unroll=8)
    cosine, sine = cos_sin((0.5 * TIME_STEP) * rows[4])
    rows[4] = cosine
    rows[5] = sine
    for k in range(4):
        arrived(copies[k + 1])

        def step(entry, carry):
            rows[k, pl.ds(entry, 1), :] = orbs[k, pl.ds(place(entry), 1), :]
            return carry

        lax.fori_loop(0, ENTRIES, step, 0, unroll=8)

    projectors_copy.wait()
    piece = 64

    def reduce(index, carry):
        at = pl.ds(pl.multiple_of(index * piece, piece), piece)
        lane = lax.broadcasted_iota(jnp.int32, (piece, LANES), 1)
        cosine, sine = rows[4, at, :], rows[5, at, :]
        inside = lane < counts[at, :]
        fields = []
        for n in range(ORBS):
            real, imag = rows[n, at, :], rows[ORBS + n, at, :]
            fields += [(n, cosine * real + sine * imag), (ORBS + n, cosine * imag - sine * real)]
        out = jnp.zeros((piece, LANES), jnp.float32)
        for f in range(4):
            masked = jnp.where(inside, projectors[f, at, :], 0.0)
            if f == 0:
                masked_ref[at, :] = masked
            for k, field in fields:
                total = jnp.sum(masked * field, axis=1, keepdims=True)
                out = jnp.where(lane == f * 4 + k, total, out)
        table[at, :] = out
        return carry

    lax.fori_loop(0, ENTRIES // piece, reduce, 0)
    turned = jnp.transpose(table[...])[:16]
    sums = lax.dot_general(
        three_parts(turned), atom_matrix(atom_ref), (((1,), (1,)), ((), ())), preferred_element_type=jnp.float32
    )
    sums = sums[:16] + sums[16:32] + sums[32:]
    for k in range(4):
        for q in range(4):
            packed[k * 4 + q : k * 4 + q + 1, :] = sums[k : k + 1, q * LANES : (q + 1) * LANES]
    slots = lax.dot_general(
        three_parts(sums), atom_matrix(slot_ref), (((1,), (1,)), ((), ())), preferred_element_type=jnp.float32
    )
    slots = slots[:16] + slots[16:32] + slots[32:]
    lane = lax.broadcasted_iota(jnp.int32, (8, LANES), 1)
    for d in range(GROUPS):
        tile = slots[:, d // 8 * LANES : (d // 8 + 1) * LANES]
        begin = d % 8 * OWNED
        upper = pltpu.roll(tile[:8], (LANES - begin) % LANES, 1)
        lower = pltpu.roll(tile[8:], (LANES - begin + OWNED) % LANES, 1)
        sent[d, 0:16, :] = packed[...]
        sent[d, 16:24, :] = jnp.where(lane < OWNED, upper, lower)


def project(orbs, potential, projectors, entry_atom, entry_block, entry_count, owner_slot):
    smem = pl.BlockSpec(memory_space=pltpu.SMEM)
    vmem = pl.BlockSpec(memory_space=pltpu.VMEM)
    hbm = pl.BlockSpec(memory_space=pltpu.HBM)
    rows = PLANES * SIZE
    return pl.pallas_call(
        project_kernel,
        out_shape=(
            jax.ShapeDtypeStruct((GROUPS, SENT, LANES), jnp.float32),
            jax.ShapeDtypeStruct((ENTRIES, LANES), jnp.float32),
        ),
        in_specs=[smem, smem, vmem, vmem, hbm, hbm, hbm],
        out_specs=(vmem, vmem),
        scratch_shapes=[
            pltpu.VMEM((4, 2 * rows, LANES), jnp.float32),
            pltpu.VMEM((2 * rows, LANES), jnp.float32),
            pltpu.VMEM((4, ENTRIES, LANES), jnp.float32),
            pltpu.VMEM((6, ENTRIES, LANES), jnp.float32),
            pltpu.VMEM((ENTRIES, LANES), jnp.int32),
            pltpu.VMEM((ENTRIES, LANES), jnp.float32),
            pltpu.VMEM((16, LANES), jnp.float32),
            pltpu.SemaphoreType.DMA((6, 2)),
        ],
        compiler_params=pltpu.CompilerParams(vmem_limit_bytes=VMEM),
        cost_estimate=pl.CostEstimate(flops=10**9, bytes_accessed=36 * 10**6, transcendentals=0),
        name="project",
    )(
        entry_block, entry_count, entry_atom.reshape(1, ENTRIES), owner_slot.reshape(1, ATOMS), orbs, potential, projectors
    )


SHIFT_STEP = 8


def shift_kernel(orbs, potential, *rest):
    out = rest[-1]
    for x in range(PLANES):
        cosine, sine = cos_sin((0.5 * TIME_STEP) * potential[x])
        real, imag = orbs[0, 0, x], orbs[1, 0, x]
        both = (cosine * real + sine * imag, cosine * imag - sine * real)
        for c in range(2):
            for d in range(SHIFT_STEP):
                for z in range(2):
                    tile = both[c][d * 8 : d * 8 + 8, z * LANES : (z + 1) * LANES]
                    out[pl.ds(d * 256 + c * 16 + z * 8 + x, 8, stride=32), :] = tile


def shift(n, orbitals, potential, *first):
    width = SHIFT_STEP * 8
    return pl.pallas_call(
        shift_kernel,
        grid=(GROUPS // SHIFT_STEP,),
        out_shape=pltpu.HBM((GROUPS * 256, LANES), jnp.float32),
        in_specs=[
            pl.BlockSpec((2, 1, PLANES, width, SIZE), lambda i: (0, n, 0, i, 0)),
            pl.BlockSpec((PLANES, width, SIZE), lambda i: (0, i, 0)),
            *[pl.BlockSpec(memory_space=pl.ANY) for _ in first],
        ],
        out_specs=pl.BlockSpec((SHIFT_STEP * 256, LANES), lambda i: (i, 0)),
        compiler_params=pltpu.CompilerParams(vmem_limit_bytes=VMEM),
        cost_estimate=pl.CostEstimate(flops=10**8, bytes_accessed=11 * 10**6, transcendentals=0),
        name=f"shift{n}",
    )(orbitals, potential, *first)


def correct_kernel(n, place, received, strength, atom_ref, masked, before, after, field, coefs, updates, sems):
    load = pltpu.make_async_copy(before, field, sems.at[0])
    load.start()
    sums = jnp.sum(received[:, 0:16, :], axis=0)
    real = sums[n * 4 : n * 4 + 4]
    imag = sums[(ORBS + n) * 4 : (ORBS + n) * 4 + 4]
    cosine, sine = cos_sin(TIME_STEP * strength[...])
    less_one = cosine - 1.0
    both = (less_one * real + sine * imag, less_one * imag - sine * real)
    coefs[...] = jnp.zeros_like(coefs)
    for c in range(2):
        for q in range(4):
            coefs[c : c + 1, q * LANES : (q + 1) * LANES] = both[c][q : q + 1]
    spread = dot(three_parts(coefs[...]), atom_matrix(atom_ref))
    spread = jnp.transpose(spread[:16] + spread[16:32] + spread[32:])
    for c in range(2):
        updates[c] = spread[:, c : c + 1] * masked[...]
    load.wait()

    def step(entry, carry):
        row = place[entry]
        at = [pl.ds(row + c * 16, 1) for c in range(2)]
        both = [field[at[c], :] + updates[c, pl.ds(entry, 1), :] for c in range(2)]
        for c in range(2):
            field[at[c], :] = both[c]
        return carry

    lax.fori_loop(0, ENTRIES, step, 0, unroll=8)
    store = pltpu.make_async_copy(field, after, sems.at[1])
    store.start()
    store.wait()


def correct(n, place, received, strength, atoms, masked, before):
    smem = pl.BlockSpec(memory_space=pltpu.SMEM)
    vmem = pl.BlockSpec(memory_space=pltpu.VMEM)
    hbm = pl.BlockSpec(memory_space=pltpu.HBM)
    return pl.pallas_call(
        functools.partial(correct_kernel, n),
        out_shape=pltpu.HBM((GROUPS * 256, LANES), jnp.float32),
        in_specs=[smem, vmem, vmem, vmem, vmem, hbm],
        out_specs=hbm,
        scratch_shapes=[
            pltpu.VMEM((GROUPS * 256, LANES), jnp.float32),
            pltpu.VMEM((16, ATOMS), jnp.float32),
            pltpu.VMEM((2, ENTRIES, LANES), jnp.float32),
            pltpu.SemaphoreType.DMA((2,)),
        ],
        input_output_aliases={5: 0},
        compiler_params=pltpu.CompilerParams(vmem_limit_bytes=24 << 20),
        cost_estimate=pl.CostEstimate(flops=5 * 10**8, bytes_accessed=20 * 10**6, transcendentals=0),
        name=f"correct{n}",
    )(place, received, strength, atoms, masked, before)


LINES_STEP = 4


def lines_kernel(n, field, left, right, *rest):
    *chunks, half_done, turned, sems = rest[-3 - len(CHUNKS) :]
    step = pl.program_id(0)
    for k in range(LINES_STEP):
        real, imag = ([field[:, k, c, z].reshape(SIZE, LANES) for z in range(2)] for c in range(2))
        both = propagate_lanes(right, real, imag)
        y = step * LINES_STEP + k
        for c in range(2):
            for z in range(2):
                half_done[c, z, y] = both[c][:, z * LANES : (z + 1) * LANES]

    @pl.when(step == pl.num_programs(0) - 1)
    def _():
        rows = turned.reshape(GROUPS, 2, PLANES * 16, LANES)
        copies = []
        for z in range(2):
            for y in range(0, 8, 2):
                real, imag = (
                    jnp.concatenate([half_done[c, z, y], half_done[c, z, y + 1]], axis=1) for c in range(2)
                )
                both = propagate_rows(left, real, imag)
                for c in range(2):
                    for k in range(2):
                        for d in range(GROUPS):
                            tile = both[c][d * 8 : d * 8 + 8, k * LANES : (k + 1) * LANES]
                            rows[d, z, pl.ds(c * 8 + y + k, 8, stride=16), :] = tile
            begin = 0
            for k, (chunk, planes) in enumerate(zip(chunks, CHUNKS)):
                part = turned.at[:, z, pl.ds(begin, planes)]
                copies.append(pltpu.make_async_copy(part, chunk.at[:, :, n, z], sems.at[z, k]))
                copies[-1].start()
                begin += planes
        for copy in copies:
            copy.wait()


def lines(n, field, left, right, before=(), first=()):
    hbm = pl.BlockSpec(memory_space=pltpu.HBM)
    return pl.pallas_call(
        functools.partial(lines_kernel, n),
        grid=(8 // LINES_STEP,),
        out_shape=tuple(
            jax.ShapeDtypeStruct((GROUPS, planes, ORBS, 2, 16, LANES), jnp.float32) for planes in CHUNKS
        ),
        in_specs=[
            pl.BlockSpec((GROUPS, LINES_STEP, 2, 2, 8, LANES), lambda i: (0, i, 0, 0, 0, 0)),
            pl.BlockSpec(left.shape, lambda i: (0, 0, 0)),
            pl.BlockSpec(right.shape, lambda i: (0, 0, 0)),
            *[hbm for _ in (*before, *first)],
        ],
        out_specs=tuple(hbm for _ in CHUNKS),
        scratch_shapes=[
            pltpu.VMEM((2, 2, 8, SIZE, LANES), jnp.float32),
            pltpu.VMEM((GROUPS, 2, PLANES, 16, LANES), jnp.float32),
            pltpu.SemaphoreType.DMA((2, len(CHUNKS))),
        ],
        input_output_aliases={3 + k: k for k in range(len(before))},
        compiler_params=pltpu.CompilerParams(vmem_limit_bytes=VMEM),
        cost_estimate=pl.CostEstimate(flops=5 * 10**9, bytes_accessed=10 * 10**6, transcendentals=0),
        name=f"lines{n}",
    )(field.reshape(GROUPS, 8, 2, 2, 8, LANES), left, right, *before, *first)


def finish_kernel(halves, band, field, potential, left, *rest):
    out, *pieces, whole = rest[-2 - BANDS * halves :]
    cosine, sine = cos_sin((0.5 * TIME_STEP) * potential[0])
    total = None
    for n in range(ORBS):
        real, imag = (
            jnp.concatenate([field[:, 0, n, z, c].reshape(SIZE, LANES) for z in range(2)], axis=1) for c in range(2)
        )
        real, imag = propagate_rows(left, real, imag)
        real, imag = cosine * real + sine * imag, cosine * imag - sine * real
        out[0, n, 0] = real
        out[1, n, 0] = imag
        square = real * real + imag * imag
        total = square if total is None else total + square
    whole[...] = total
    rows = SIZE // BANDS // halves
    for k, piece in enumerate(pieces):
        begin = (band[0] + k // halves) % BANDS * halves + k % halves
        piece[0] = whole[pl.ds(pl.multiple_of(begin * rows, rows), rows), :]


def finish(planes, begin, halves, band, field, potential, left, before=(), first=()):
    rows = SIZE // BANDS // halves
    return pl.pallas_call(
        functools.partial(finish_kernel, halves),
        grid=(planes,),
        out_shape=(
            jax.ShapeDtypeStruct((2, ORBS, PLANES, SIZE, SIZE), jnp.float32),
            *[jax.ShapeDtypeStruct((planes, rows, SIZE), jnp.float32) for _ in range(BANDS * halves)],
        ),
        in_specs=[
            pl.BlockSpec(memory_space=pltpu.SMEM),
            pl.BlockSpec((GROUPS, 1, ORBS, 2, 2, 8, LANES), lambda i: (0, i, 0, 0, 0, 0, 0)),
            pl.BlockSpec((1, SIZE, SIZE), lambda i: (i + begin, 0, 0)),
            pl.BlockSpec(left.shape, lambda i: (0, 0, 0)),
            *[pl.BlockSpec(memory_space=pl.ANY) for _ in (*before, *first)],
        ],
        out_specs=(
            pl.BlockSpec((2, ORBS, 1, SIZE, SIZE), lambda i: (0, 0, i + begin, 0, 0)),
            *[pl.BlockSpec((1, rows, SIZE), lambda i: (i, 0, 0)) for _ in range(BANDS * halves)],
        ),
        scratch_shapes=[pltpu.VMEM((SIZE, SIZE), jnp.float32)],
        input_output_aliases={4 + k: k for k in range(len(before))},
        compiler_params=pltpu.CompilerParams(vmem_limit_bytes=VMEM),
        cost_estimate=pl.CostEstimate(flops=10**9 * planes, bytes_accessed=3 * 10**6 * planes, transcendentals=0),
        name=f"finish{begin}",
    )(band, field.reshape(GROUPS, planes, ORBS, 2, 2, 8, LANES), potential, left, *before, *first)


def collect_kernel(owners, band, *refs):
    out, mark = refs[-2:]
    mark[...] = jnp.zeros_like(mark)
    rows = SIZE // BANDS
    for piece, (owner, offset) in zip(refs, owners):
        row = pl.multiple_of((band[0] + owner) % BANDS * rows, rows)
        out[0, pl.ds(pl.multiple_of(row + offset, rows // 2), piece.shape[1]), :] = piece[0]


def collect(begin, band, pieces, owners, *before):
    return pl.pallas_call(
        functools.partial(collect_kernel, owners),
        grid=(pieces[0].shape[0],),
        out_shape=(
            jax.ShapeDtypeStruct((PLANES, SIZE, SIZE), jnp.float32),
            jax.ShapeDtypeStruct((8, LANES), jnp.float32),
        ),
        in_specs=[
            pl.BlockSpec(memory_space=pltpu.SMEM),
            *[pl.BlockSpec((1, piece.shape[1], SIZE), lambda i: (i, 0, 0)) for piece in pieces],
            *[pl.BlockSpec(memory_space=pltpu.HBM) for _ in before],
        ],
        out_specs=(
            pl.BlockSpec((1, SIZE, SIZE), lambda i: (i + begin, 0, 0)),
            pl.BlockSpec((8, LANES), lambda i: (0, 0)),
        ),
        input_output_aliases={1 + len(pieces) + k: k for k in range(len(before))},
        compiler_params=pltpu.CompilerParams(vmem_limit_bytes=VMEM if begin == 0 else 16 << 20),
        cost_estimate=pl.CostEstimate(flops=0, bytes_accessed=3 * 10**6, transcendentals=0),
        name=f"collect{begin}",
    )(band, *pieces, *before)


def onward(array, steps):
    return lax.ppermute(array, "band", [(b, (b + steps) % BANDS) for b in range(BANDS)])


def ring_reduce(pieces):
    own_low, own_high, next_low, next_high, across_low, across_high, last_low, last_high = pieces
    from_last = onward(across_low, 1)
    from_next = onward(across_high, 3)
    high = own_high + onward(next_high, 1)
    low = own_low + onward(last_low, 3)
    return low + onward(next_low + from_last, 1), high + onward(last_high + from_next, 3)


def ring_gather(low, high):
    last_low, next_high = onward(low, 1), onward(high, 3)
    last_high, next_low = onward(high, 1), onward(low, 3)
    pieces = low, high, last_low, last_high, next_low, next_high, onward(last_low, 1), onward(next_high, 3)
    half = SIZE // BANDS // 2
    return pieces, tuple((owner, offset) for owner in (0, 3, 1, 2) for offset in (0, half))


def add_kernel(own, from_last, across, from_next, *rest):
    rest[-1][...] = own[...] + from_last[...] + across[...] + from_next[...]


def direct_reduce(pieces, first):
    parts = [pieces[0], *[onward(pieces[k], k) for k in range(1, BANDS)]]
    return pl.pallas_call(
        add_kernel,
        out_shape=jax.ShapeDtypeStruct(pieces[0].shape, jnp.float32),
        in_specs=[
            *[pl.BlockSpec(memory_space=pltpu.VMEM) for _ in parts],
            *[pl.BlockSpec(memory_space=pltpu.HBM) for _ in first],
        ],
        out_specs=pl.BlockSpec(memory_space=pltpu.VMEM),
        compiler_params=pltpu.CompilerParams(vmem_limit_bytes=16 << 20),
        cost_estimate=pl.CostEstimate(flops=10**6, bytes_accessed=10**6, transcendentals=0),
        name="add",
    )(*parts, *first)


def direct_gather(total):
    return (total, *[onward(total, k) for k in range(1, BANDS)]), ((0, 0), (3, 0), (2, 0), (1, 0))


def exchange(array):
    return lax.all_to_all(array, "grid", split_axis=0, concat_axis=0, tiled=True)


def body(left, right, orbitals, potential, projectors, entry_atom, entry_block, entry_count, owner_slot, strength):
    atom_ids = jnp.arange(ATOMS, dtype=jnp.int32)
    rows = PLANES * SIZE
    band = lax.axis_index("band").astype(jnp.int32).reshape(1)
    sent, masked = project(
        orbitals.reshape(2 * ORBS, rows, SIZE), potential.reshape(rows, SIZE), projectors,
        entry_atom, entry_block, entry_count, owner_slot,
    )
    received = exchange(sent)
    x, y, z = entry_block // 512, (entry_block // 2) % SIZE, entry_block % 2
    place = y * 32 + z * 8 + x
    in_slot = owner_slot[:, None] == atom_ids[None, :]
    strength_atom = jnp.sum(jnp.where(in_slot, strength[None, :], 0.0), axis=1).reshape(4, LANES)
    atoms = entry_atom.reshape(1, ENTRIES)
    pencils, sent = [], ()
    for n in range(ORBS):
        shifted = shift(n, orbitals, potential, *sent)
        fixed = correct(n, place, received, strength_atom, atoms, masked, shifted)
        pencils.append(exchange(fixed.reshape(GROUPS, 256, LANES)))
        sent = (fixed,)
    mine = jnp.sum(received[:, 16:], axis=0)
    mine = jnp.concatenate([mine[:, :OWNED], mine[:, OWNED : 2 * OWNED]], axis=0).reshape(4, 2 * ORBS, OWNED)
    strength_mine = lax.dynamic_slice_in_dim(strength, lax.axis_index("grid") * OWNED, OWNED)
    forces = -2.0 * strength_mine * jnp.sum(mine[0][None] * mine[1:], axis=1)
    forces = sum([onward(forces, k) for k in range(1, BANDS)], forces)

    back = lines(0, pencils[0], left, right)
    back = lines(1, pencils[1], left, right, back, (forces,))
    out, density, ready, marks, begin = (), (), (), (), 0
    for k, planes in enumerate(CHUNKS):
        field = exchange(back[k])
        made, *pieces = finish(planes, begin, 2 if k == 0 else 1, band, field, potential, left, out, ready)
        out = (made,)
        if k == 0:
            sums, owners = ring_gather(*ring_reduce(pieces))
            ready = sums[2:]
        else:
            sums, owners = direct_gather(direct_reduce(pieces, marks))
        made, mark = collect(begin, band, sums, owners, *density)
        density, marks = (made,), (mark,)
        begin += planes
    return out[0], density[0], forces


def solution(mesh):
    left, right = propagator_tables()
    in_specs = (
        P(None, "band", "grid", None, None),
        P("grid", None, None),
        P(None, "grid", None),
        P("grid"),
        P("grid"),
        P("grid"),
        P(),
        P(),
    )
    out_specs = (P(None, "band", "grid", None, None), P("grid", None, None), P(None, "grid"))

    def run(*args):
        return body(jnp.asarray(left), jnp.asarray(right), *args)

    return jax.shard_map(run, mesh=mesh, in_specs=in_specs, out_specs=out_specs, check_vma=False)
```

```python
import functools
import math

import jax
import jax.numpy as jnp
import ml_dtypes
import numpy as np
from jax import lax
from jax.experimental import pallas as pl
from jax.experimental.pallas import tpu as pltpu
from jax.sharding import PartitionSpec as P

SIZE = 256
HALF = SIZE // 2
LANES = 128
TIME_STEP = 4.0
HIGHEST = lax.Precision.HIGHEST
ORBS = 2
EARLY = (1,)
BANDS = 4
PLANES = 8
GROUPS = 32
ENTRIES = 512
ATOMS = 512
OWNED = ATOMS // GROUPS
CHUNKS = (5, 3)
VMEM = 56 << 20
SENT = 24


def propagator_tables():
    index = np.arange(SIZE)
    freq = np.where(index < HALF, index, index - SIZE)
    wave = freq * (2.0 * math.pi / SIZE)
    line = np.fft.ifft(np.exp(-0.5j * TIME_STEP * wave * wave))
    full = line[(index[:, None] - index[None, :]) % SIZE]
    left = []
    for sign in (1.0, -1.0):
        half = 0.5 * (full[:HALF, :HALF] + sign * full[:HALF, HALF:])
        real = np.block([[half.real, -half.imag], [half.imag, half.real]]).astype(np.float32)
        high = real.astype(ml_dtypes.bfloat16)
        low = (real - high.astype(np.float32)).astype(ml_dtypes.bfloat16)
        left.append(np.concatenate([high, high, low], axis=1))
    left = np.stack(left)
    return left, np.ascontiguousarray(np.swapaxes(left, 1, 2))


def cos_sin(angle):
    turns = jnp.floor(angle * (2.0 / math.pi) + 0.5)
    rest = angle - turns * 1.5703125
    rest = rest - turns * 4.837512969970703125e-4
    rest = rest - turns * 7.54978995489188216e-8
    square = rest * rest
    sine = ((-1.9515295891e-4 * square + 8.3321608736e-3) * square - 1.6666654611e-1) * square * rest + rest
    cosine = ((2.443315711809948e-5 * square - 1.388731625493765e-3) * square + 4.166664568298827e-2) * (
        square * square
    ) - 0.5 * square + 1.0
    quarter = turns.astype(jnp.int32)
    odd = (quarter & 1) == 1
    cos_out = jnp.where(odd, sine, cosine)
    sin_out = jnp.where(odd, cosine, sine)
    cos_out = jnp.where(((quarter + 1) & 2) == 2, -cos_out, cos_out)
    sin_out = jnp.where((quarter & 2) == 2, -sin_out, sin_out)
    return cos_out, sin_out


def split(values, axis):
    high = values.astype(jnp.bfloat16)
    low = (values - high.astype(jnp.float32)).astype(jnp.bfloat16)
    return jnp.concatenate([high, low, high], axis=axis)


def three_parts(values):
    high = values.astype(jnp.bfloat16)
    rest = values - high.astype(jnp.float32)
    middle = rest.astype(jnp.bfloat16)
    low = (rest - middle.astype(jnp.float32)).astype(jnp.bfloat16)
    return jnp.concatenate([high, middle, low], axis=0)


def dot(left, right):
    return jnp.dot(left, right, preferred_element_type=jnp.float32)


def propagate_rows(table, real, imag):
    plus = jnp.concatenate([real[:HALF] + real[HALF:], imag[:HALF] + imag[HALF:]], axis=0)
    minus = jnp.concatenate([real[:HALF] - real[HALF:], imag[:HALF] - imag[HALF:]], axis=0)
    plus = dot(table[0], split(plus, 0))
    minus = dot(table[1], split(minus, 0))
    low, high = plus + minus, plus - minus
    return (
        jnp.concatenate([low[:HALF], high[:HALF]], axis=0),
        jnp.concatenate([low[HALF:], high[HALF:]], axis=0),
    )


def propagate_lanes(table, real, imag):
    plus = jnp.concatenate([real[0] + real[1], imag[0] + imag[1]], axis=1)
    minus = jnp.concatenate([real[0] - real[1], imag[0] - imag[1]], axis=1)
    plus = dot(split(plus, 1), table[0])
    minus = dot(split(minus, 1), table[1])
    low, high = plus + minus, plus - minus
    return (
        jnp.concatenate([low[:, :HALF], high[:, :HALF]], axis=1),
        jnp.concatenate([low[:, HALF:], high[:, HALF:]], axis=1),
    )


def atom_matrix(atom_ref):
    atoms = lax.broadcasted_iota(jnp.int32, (ATOMS, ENTRIES), 0)
    return jnp.where(atoms == atom_ref[...], 1.0, 0.0).astype(jnp.bfloat16)


def project_kernel(
    block, count, atom_ref, slot_ref, orbs_hbm, potential_hbm, projectors_hbm, sent, masked_ref,
    orbs, potential, projectors, rows, counts, table, packed, sems,
):
    half_rows = PLANES * SIZE

    def load(source, into, sem):
        return [
            pltpu.make_async_copy(
                source.at[:, pl.ds(z * LANES, LANES)], into.at[pl.ds(z * half_rows, half_rows)], sem.at[z]
            )
            for z in range(2)
        ]

    copies = [load(potential_hbm, potential, sems.at[4])]
    copies += [load(orbs_hbm.at[k], orbs.at[k], sems.at[k]) for k in range(4)]
    projectors_copy = pltpu.make_async_copy(projectors_hbm, projectors, sems.at[5, 0])
    for pair in copies:
        for copy in pair:
            copy.start()
    projectors_copy.start()

    def arrived(pair):
        for copy in pair:
            copy.wait()

    def place(entry):
        at = block[entry]
        return (at & 1) * half_rows + lax.shift_right_logical(at, 1)

    arrived(copies[0])

    def first(entry, carry):
        rows[4, pl.ds(entry, 1), :] = potential[pl.ds(place(entry), 1), :]
        counts[pl.ds(entry, 1), :] = jnp.full((1, LANES), count[entry], jnp.int32)
        return carry

    lax.fori_loop(0, ENTRIES, first, 0, unroll=8)
    cosine, sine = cos_sin((0.5 * TIME_STEP) * rows[4])
    rows[4] = cosine
    rows[5] = sine
    for k in range(4):
        arrived(copies[k + 1])

        def step(entry, carry):
            rows[k, pl.ds(entry, 1), :] = orbs[k, pl.ds(place(entry), 1), :]
            return carry

        lax.fori_loop(0, ENTRIES, step, 0, unroll=8)

    projectors_copy.wait()
    piece = 64

    def reduce(index, carry):
        at = pl.ds(pl.multiple_of(index * piece, piece), piece)
        lane = lax.broadcasted_iota(jnp.int32, (piece, LANES), 1)
        cosine, sine = rows[4, at, :], rows[5, at, :]
        inside = lane < counts[at, :]
        fields = []
        for n in range(ORBS):
            real, imag = rows[n, at, :], rows[ORBS + n, at, :]
            fields += [(n, cosine * real + sine * imag), (ORBS + n, cosine * imag - sine * real)]
        out = jnp.zeros((piece, LANES), jnp.float32)
        for f in range(4):
            masked = jnp.where(inside, projectors[f, at, :], 0.0)
            if f == 0:
                masked_ref[at, :] = masked
            for k, field in fields:
                total = jnp.sum(masked * field, axis=1, keepdims=True)
                out = jnp.where(lane == f * 4 + k, total, out)
        table[at, :] = out
        return carry

    lax.fori_loop(0, ENTRIES // piece, reduce, 0)
    turned = jnp.transpose(table[...])[:16]
    sums = lax.dot_general(
        three_parts(turned), atom_matrix(atom_ref), (((1,), (1,)), ((), ())), preferred_element_type=jnp.float32
    )
    sums = sums[:16] + sums[16:32] + sums[32:]
    for k in range(4):
        for q in range(4):
            packed[k * 4 + q : k * 4 + q + 1, :] = sums[k : k + 1, q * LANES : (q + 1) * LANES]
    slots = lax.dot_general(
        three_parts(sums), atom_matrix(slot_ref), (((1,), (1,)), ((), ())), preferred_element_type=jnp.float32
    )
    slots = slots[:16] + slots[16:32] + slots[32:]
    lane = lax.broadcasted_iota(jnp.int32, (8, LANES), 1)
    for d in range(GROUPS):
        tile = slots[:, d // 8 * LANES : (d // 8 + 1) * LANES]
        begin = d % 8 * OWNED
        upper = pltpu.roll(tile[:8], (LANES - begin) % LANES, 1)
        lower = pltpu.roll(tile[8:], (LANES - begin + OWNED) % LANES, 1)
        sent[d, 0:16, :] = packed[...]
        sent[d, 16:24, :] = jnp.where(lane < OWNED, upper, lower)


def project(orbs, potential, projectors, entry_atom, entry_block, entry_count, owner_slot):
    smem = pl.BlockSpec(memory_space=pltpu.SMEM)
    vmem = pl.BlockSpec(memory_space=pltpu.VMEM)
    hbm = pl.BlockSpec(memory_space=pltpu.HBM)
    rows = PLANES * SIZE
    return pl.pallas_call(
        project_kernel,
        out_shape=(
            jax.ShapeDtypeStruct((GROUPS, SENT, LANES), jnp.float32),
            jax.ShapeDtypeStruct((ENTRIES, LANES), jnp.float32),
        ),
        in_specs=[smem, smem, vmem, vmem, hbm, hbm, hbm],
        out_specs=(vmem, vmem),
        scratch_shapes=[
            pltpu.VMEM((4, 2 * rows, LANES), jnp.float32),
            pltpu.VMEM((2 * rows, LANES), jnp.float32),
            pltpu.VMEM((4, ENTRIES, LANES), jnp.float32),
            pltpu.VMEM((6, ENTRIES, LANES), jnp.float32),
            pltpu.VMEM((ENTRIES, LANES), jnp.int32),
            pltpu.VMEM((ENTRIES, LANES), jnp.float32),
            pltpu.VMEM((16, LANES), jnp.float32),
            pltpu.SemaphoreType.DMA((6, 2)),
        ],
        compiler_params=pltpu.CompilerParams(vmem_limit_bytes=VMEM),
        cost_estimate=pl.CostEstimate(flops=10**9, bytes_accessed=36 * 10**6, transcendentals=0),
        name="project",
    )(
        entry_block, entry_count, entry_atom.reshape(1, ENTRIES), owner_slot.reshape(1, ATOMS), orbs, potential, projectors
    )


SHIFT_STEP = 8


def shift_kernel(orbs, potential, *rest):
    out = rest[-1]
    for x in range(PLANES):
        cosine, sine = cos_sin((0.5 * TIME_STEP) * potential[x])
        real, imag = orbs[0, 0, x], orbs[1, 0, x]
        both = (cosine * real + sine * imag, cosine * imag - sine * real)
        for c in range(2):
            for d in range(SHIFT_STEP):
                for z in range(2):
                    tile = both[c][d * 8 : d * 8 + 8, z * LANES : (z + 1) * LANES]
                    out[pl.ds(d * 256 + c * 16 + z * 8 + x, 8, stride=32), :] = tile


def shift(n, orbitals, potential, *first):
    width = SHIFT_STEP * 8
    return pl.pallas_call(
        shift_kernel,
        grid=(GROUPS // SHIFT_STEP,),
        out_shape=pltpu.HBM((GROUPS * 256, LANES), jnp.float32),
        in_specs=[
            pl.BlockSpec((2, 1, PLANES, width, SIZE), lambda i: (0, n, 0, i, 0)),
            pl.BlockSpec((PLANES, width, SIZE), lambda i: (0, i, 0)),
            *[pl.BlockSpec(memory_space=pl.ANY) for _ in first],
        ],
        out_specs=pl.BlockSpec((SHIFT_STEP * 256, LANES), lambda i: (i, 0)),
        compiler_params=pltpu.CompilerParams(vmem_limit_bytes=VMEM),
        cost_estimate=pl.CostEstimate(flops=10**8, bytes_accessed=11 * 10**6, transcendentals=0),
        name=f"shift{n}",
    )(orbitals, potential, *first)


def correct_kernel(n, place, received, strength, atom_ref, masked, right, before, after, field, coefs, updates, sems):
    load = pltpu.make_async_copy(before, field, sems.at[0])
    load.start()
    sums = jnp.sum(received[:, 0:16, :], axis=0)
    real = sums[n * 4 : n * 4 + 4]
    imag = sums[(ORBS + n) * 4 : (ORBS + n) * 4 + 4]
    cosine, sine = cos_sin(TIME_STEP * strength[...])
    less_one = cosine - 1.0
    both = (less_one * real + sine * imag, less_one * imag - sine * real)
    coefs[...] = jnp.zeros_like(coefs)
    for c in range(2):
        for q in range(4):
            coefs[c : c + 1, q * LANES : (q + 1) * LANES] = both[c][q : q + 1]
    spread = dot(three_parts(coefs[...]), atom_matrix(atom_ref))
    spread = jnp.transpose(spread[:16] + spread[16:32] + spread[32:])
    for c in range(2):
        updates[c] = spread[:, c : c + 1] * masked[...]
    load.wait()

    def step(entry, carry):
        row = place[entry]
        at = [pl.ds(row + c * 16, 1) for c in range(2)]
        both = [field[at[c], :] + updates[c, pl.ds(entry, 1), :] for c in range(2)]
        for c in range(2):
            field[at[c], :] = both[c]
        return carry

    lax.fori_loop(0, ENTRIES, step, 0, unroll=8)
    if n in EARLY:
        tiles = field.reshape(GROUPS * 8, 2, 2, 8, LANES)

        def z_lines(index, carry):
            at = pl.ds(index * 32, 32)
            real, imag = ([tiles[at, c, z].reshape(SIZE, LANES) for z in range(2)] for c in range(2))
            both = propagate_lanes(right, real, imag)
            for c in range(2):
                for z in range(2):
                    tiles[at, c, z] = both[c][:, z * LANES : (z + 1) * LANES].reshape(32, 8, LANES)
            return carry

        lax.fori_loop(0, GROUPS * 8 // 32, z_lines, 0)
    store = pltpu.make_async_copy(field, after, sems.at[1])
    store.start()
    store.wait()


def correct(n, place, received, strength, atoms, masked, right, before):
    smem = pl.BlockSpec(memory_space=pltpu.SMEM)
    vmem = pl.BlockSpec(memory_space=pltpu.VMEM)
    hbm = pl.BlockSpec(memory_space=pltpu.HBM)
    return pl.pallas_call(
        functools.partial(correct_kernel, n),
        out_shape=pltpu.HBM((GROUPS * 256, LANES), jnp.float32),
        in_specs=[smem, vmem, vmem, vmem, vmem, vmem, hbm],
        out_specs=hbm,
        scratch_shapes=[
            pltpu.VMEM((GROUPS * 256, LANES), jnp.float32),
            pltpu.VMEM((16, ATOMS), jnp.float32),
            pltpu.VMEM((2, ENTRIES, LANES), jnp.float32),
            pltpu.SemaphoreType.DMA((2,)),
        ],
        input_output_aliases={6: 0},
        compiler_params=pltpu.CompilerParams(vmem_limit_bytes=24 << 20),
        cost_estimate=pl.CostEstimate(flops=5 * 10**8, bytes_accessed=20 * 10**6, transcendentals=0),
        name=f"correct{n}",
    )(place, received, strength, atoms, masked, right if n in EARLY else right[:, :8, :LANES], before)


LINES_STEP = 4


def lines_kernel(n, field, left, right, *rest):
    *chunks, half_done, turned, sems = rest[-3 - len(CHUNKS) :]
    step = pl.program_id(0)
    last = step == pl.num_programs(0) - 1
    rows = turned.reshape(GROUPS, 2, PLANES * 16, LANES)

    def x_lines(z, y, real, imag):
        both = propagate_rows(left, jnp.concatenate(real, axis=1), jnp.concatenate(imag, axis=1))
        for c in range(2):
            for k in range(2):
                for d in range(GROUPS):
                    tile = both[c][d * 8 : d * 8 + 8, k * LANES : (k + 1) * LANES]
                    rows[d, z, pl.ds(c * 8 + y + k, 8, stride=16), :] = tile

    def copies(z):
        begin = 0
        for k, (chunk, planes) in enumerate(zip(chunks, CHUNKS)):
            part = turned.at[:, z, pl.ds(begin, planes)]
            yield pltpu.make_async_copy(part, chunk.at[:, :, n, z], sems.at[z, k])
            begin += planes

    if n in EARLY:
        for z in range(2):
            for k in range(0, LINES_STEP, 2):
                parts = ([field[:, k + j, c, z].reshape(SIZE, LANES) for j in range(2)] for c in range(2))
                x_lines(z, step * LINES_STEP + k, *parts)

            @pl.when(last)
            def _():
                for copy in copies(z):
                    copy.start()

    else:
        for k in range(LINES_STEP):
            real, imag = ([field[:, k, c, z].reshape(SIZE, LANES) for z in range(2)] for c in range(2))
            both = propagate_lanes(right, real, imag)
            y = step * LINES_STEP + k
            for c in range(2):
                for z in range(2):
                    half_done[c, z, y] = both[c][:, z * LANES : (z + 1) * LANES]

        @pl.when(last)
        def _():
            for z in range(2):
                for y in range(0, 8, 2):
                    x_lines(z, y, *([half_done[c, z, y + j] for j in range(2)] for c in range(2)))
                for copy in copies(z):
                    copy.start()

    @pl.when(last)
    def _():
        for z in range(2):
            for copy in copies(z):
                copy.wait()


def lines(n, field, left, right, before=(), first=()):
    hbm = pl.BlockSpec(memory_space=pltpu.HBM)
    return pl.pallas_call(
        functools.partial(lines_kernel, n),
        grid=(8 // LINES_STEP,),
        out_shape=tuple(
            jax.ShapeDtypeStruct((GROUPS, planes, ORBS, 2, 16, LANES), jnp.float32) for planes in CHUNKS
        ),
        in_specs=[
            pl.BlockSpec((GROUPS, LINES_STEP, 2, 2, 8, LANES), lambda i: (0, i, 0, 0, 0, 0)),
            pl.BlockSpec(left.shape, lambda i: (0, 0, 0)),
            pl.BlockSpec(right.shape, lambda i: (0, 0, 0)),
            *[hbm for _ in (*before, *first)],
        ],
        out_specs=tuple(hbm for _ in CHUNKS),
        scratch_shapes=[
            pltpu.VMEM((2, 2, 8, SIZE, LANES), jnp.float32),
            pltpu.VMEM((GROUPS, 2, PLANES, 16, LANES), jnp.float32),
            pltpu.SemaphoreType.DMA((2, len(CHUNKS))),
        ],
        input_output_aliases={3 + k: k for k in range(len(before))},
        compiler_params=pltpu.CompilerParams(vmem_limit_bytes=VMEM),
        cost_estimate=pl.CostEstimate(flops=5 * 10**9, bytes_accessed=10 * 10**6, transcendentals=0),
        name=f"lines{n}",
    )(field.reshape(GROUPS, 8, 2, 2, 8, LANES), left, right, *before, *first)


def finish_kernel(halves, band, field, potential, left, *rest):
    out, *pieces, whole = rest[-2 - BANDS * halves :]
    cosine, sine = cos_sin((0.5 * TIME_STEP) * potential[0])
    total = None
    for n in range(ORBS):
        real, imag = (
            jnp.concatenate([field[:, 0, n, z, c].reshape(SIZE, LANES) for z in range(2)], axis=1) for c in range(2)
        )
        real, imag = propagate_rows(left, real, imag)
        real, imag = cosine * real + sine * imag, cosine * imag - sine * real
        out[0, n, 0] = real
        out[1, n, 0] = imag
        square = real * real + imag * imag
        total = square if total is None else total + square
    whole[...] = total
    rows = SIZE // BANDS // halves
    for k, piece in enumerate(pieces):
        begin = (band[0] + k // halves) % BANDS * halves + k % halves
        piece[0] = whole[pl.ds(pl.multiple_of(begin * rows, rows), rows), :]


def finish(planes, begin, halves, band, field, potential, left, before=(), first=()):
    rows = SIZE // BANDS // halves
    return pl.pallas_call(
        functools.partial(finish_kernel, halves),
        grid=(planes,),
        out_shape=(
            jax.ShapeDtypeStruct((2, ORBS, PLANES, SIZE, SIZE), jnp.float32),
            *[jax.ShapeDtypeStruct((planes, rows, SIZE), jnp.float32) for _ in range(BANDS * halves)],
        ),
        in_specs=[
            pl.BlockSpec(memory_space=pltpu.SMEM),
            pl.BlockSpec((GROUPS, 1, ORBS, 2, 2, 8, LANES), lambda i: (0, i, 0, 0, 0, 0, 0)),
            pl.BlockSpec((1, SIZE, SIZE), lambda i: (i + begin, 0, 0)),
            pl.BlockSpec(left.shape, lambda i: (0, 0, 0)),
            *[pl.BlockSpec(memory_space=pl.ANY) for _ in (*before, *first)],
        ],
        out_specs=(
            pl.BlockSpec((2, ORBS, 1, SIZE, SIZE), lambda i: (0, 0, i + begin, 0, 0)),
            *[pl.BlockSpec((1, rows, SIZE), lambda i: (i, 0, 0)) for _ in range(BANDS * halves)],
        ),
        scratch_shapes=[pltpu.VMEM((SIZE, SIZE), jnp.float32)],
        input_output_aliases={4 + k: k for k in range(len(before))},
        compiler_params=pltpu.CompilerParams(vmem_limit_bytes=VMEM),
        cost_estimate=pl.CostEstimate(flops=10**9 * planes, bytes_accessed=3 * 10**6 * planes, transcendentals=0),
        name=f"finish{begin}",
    )(band, field.reshape(GROUPS, planes, ORBS, 2, 2, 8, LANES), potential, left, *before, *first)


def collect_kernel(owners, band, *refs):
    out, mark = refs[-2:]
    mark[...] = jnp.zeros_like(mark)
    rows = SIZE // BANDS
    for piece, (owner, offset) in zip(refs, owners):
        row = pl.multiple_of((band[0] + owner) % BANDS * rows, rows)
        out[0, pl.ds(pl.multiple_of(row + offset, rows // 2), piece.shape[1]), :] = piece[0]


def collect(begin, band, pieces, owners, *before):
    return pl.pallas_call(
        functools.partial(collect_kernel, owners),
        grid=(pieces[0].shape[0],),
        out_shape=(
            jax.ShapeDtypeStruct((PLANES, SIZE, SIZE), jnp.float32),
            jax.ShapeDtypeStruct((8, LANES), jnp.float32),
        ),
        in_specs=[
            pl.BlockSpec(memory_space=pltpu.SMEM),
            *[pl.BlockSpec((1, piece.shape[1], SIZE), lambda i: (i, 0, 0)) for piece in pieces],
            *[pl.BlockSpec(memory_space=pltpu.HBM) for _ in before],
        ],
        out_specs=(
            pl.BlockSpec((1, SIZE, SIZE), lambda i: (i + begin, 0, 0)),
            pl.BlockSpec((8, LANES), lambda i: (0, 0)),
        ),
        input_output_aliases={1 + len(pieces) + k: k for k in range(len(before))},
        compiler_params=pltpu.CompilerParams(vmem_limit_bytes=VMEM if begin == 0 else 16 << 20),
        cost_estimate=pl.CostEstimate(flops=0, bytes_accessed=3 * 10**6, transcendentals=0),
        name=f"collect{begin}",
    )(band, *pieces, *before)


def onward(array, steps):
    return lax.ppermute(array, "band", [(b, (b + steps) % BANDS) for b in range(BANDS)])


def ring_reduce(pieces):
    own_low, own_high, next_low, next_high, across_low, across_high, last_low, last_high = pieces
    from_last = onward(across_low, 1)
    from_next = onward(across_high, 3)
    high = own_high + onward(next_high, 1)
    low = own_low + onward(last_low, 3)
    return low + onward(next_low + from_last, 1), high + onward(last_high + from_next, 3)


def ring_gather(low, high):
    last_low, next_high = onward(low, 1), onward(high, 3)
    last_high, next_low = onward(high, 1), onward(low, 3)
    pieces = low, high, last_low, last_high, next_low, next_high, onward(last_low, 1), onward(next_high, 3)
    half = SIZE // BANDS // 2
    return pieces, tuple((owner, offset) for owner in (0, 3, 1, 2) for offset in (0, half))


def add_kernel(own, from_last, across, from_next, *rest):
    rest[-1][...] = own[...] + from_last[...] + across[...] + from_next[...]


def direct_reduce(pieces, first):
    parts = [pieces[0], *[onward(pieces[k], k) for k in range(1, BANDS)]]
    return pl.pallas_call(
        add_kernel,
        out_shape=jax.ShapeDtypeStruct(pieces[0].shape, jnp.float32),
        in_specs=[
            *[pl.BlockSpec(memory_space=pltpu.VMEM) for _ in parts],
            *[pl.BlockSpec(memory_space=pltpu.HBM) for _ in first],
        ],
        out_specs=pl.BlockSpec(memory_space=pltpu.VMEM),
        compiler_params=pltpu.CompilerParams(vmem_limit_bytes=16 << 20),
        cost_estimate=pl.CostEstimate(flops=10**6, bytes_accessed=10**6, transcendentals=0),
        name="add",
    )(*parts, *first)


def direct_gather(total):
    return (total, *[onward(total, k) for k in range(1, BANDS)]), ((0, 0), (3, 0), (2, 0), (1, 0))


def exchange(array):
    return lax.all_to_all(array, "grid", split_axis=0, concat_axis=0, tiled=True)


def body(left, right, orbitals, potential, projectors, entry_atom, entry_block, entry_count, owner_slot, strength):
    atom_ids = jnp.arange(ATOMS, dtype=jnp.int32)
    rows = PLANES * SIZE
    band = lax.axis_index("band").astype(jnp.int32).reshape(1)
    sent, masked = project(
        orbitals.reshape(2 * ORBS, rows, SIZE), potential.reshape(rows, SIZE), projectors,
        entry_atom, entry_block, entry_count, owner_slot,
    )
    received = exchange(sent)
    x, y, z = entry_block // 512, (entry_block // 2) % SIZE, entry_block % 2
    place = y * 32 + z * 8 + x
    in_slot = owner_slot[:, None] == atom_ids[None, :]
    strength_atom = jnp.sum(jnp.where(in_slot, strength[None, :], 0.0), axis=1).reshape(4, LANES)
    atoms = entry_atom.reshape(1, ENTRIES)
    pencils, sent = [], ()
    for n in range(ORBS):
        shifted = shift(n, orbitals, potential, *sent)
        fixed = correct(n, place, received, strength_atom, atoms, masked, right, shifted)
        pencils.append(exchange(fixed.reshape(GROUPS, 256, LANES)))
        sent = (fixed,)
    mine = jnp.sum(received[:, 16:], axis=0)
    mine = jnp.concatenate([mine[:, :OWNED], mine[:, OWNED : 2 * OWNED]], axis=0).reshape(4, 2 * ORBS, OWNED)
    strength_mine = lax.dynamic_slice_in_dim(strength, lax.axis_index("grid") * OWNED, OWNED)
    forces = -2.0 * strength_mine * jnp.sum(mine[0][None] * mine[1:], axis=1)
    forces = sum([onward(forces, k) for k in range(1, BANDS)], forces)

    back = lines(0, pencils[0], left, right)
    back = lines(1, pencils[1], left, right, back, (forces,))
    out, density, ready, marks, begin = (), (), (), (), 0
    for k, planes in enumerate(CHUNKS):
        field = exchange(back[k])
        made, *pieces = finish(planes, begin, 2 if k == 0 else 1, band, field, potential, left, out, ready)
        out = (made,)
        if k == 0:
            sums, owners = ring_gather(*ring_reduce(pieces))
            ready = sums[2:]
        else:
            sums, owners = direct_gather(direct_reduce(pieces, marks))
        made, mark = collect(begin, band, sums, owners, *density)
        density, marks = (made,), (mark,)
        begin += planes
    return out[0], density[0], forces


def solution(mesh):
    left, right = propagator_tables()
    in_specs = (
        P(None, "band", "grid", None, None),
        P("grid", None, None),
        P(None, "grid", None),
        P("grid"),
        P("grid"),
        P("grid"),
        P(),
        P(),
    )
    out_specs = (P(None, "band", "grid", None, None), P("grid", None, None), P(None, "grid"))

    def run(*args):
        return body(jnp.asarray(left), jnp.asarray(right), *args)

    return jax.shard_map(run, mesh=mesh, in_specs=in_specs, out_specs=out_specs, check_vma=False)
```

```python
import functools
import math

import jax
import jax.numpy as jnp
import ml_dtypes
import numpy as np
from jax import lax
from jax.experimental import pallas as pl
from jax.experimental.pallas import tpu as pltpu
from jax.sharding import PartitionSpec as P

SIZE = 256
HALF = SIZE // 2
LANES = 128
TIME_STEP = 4.0
HIGHEST = lax.Precision.HIGHEST
ORBS = 2
EARLY = (1,)
BANDS = 4
PLANES = 8
GROUPS = 32
ENTRIES = 512
ATOMS = 512
OWNED = ATOMS // GROUPS
CHUNKS = (5, 3)
VMEM = 56 << 20
SENT = 24


def propagator_tables():
    index = np.arange(SIZE)
    freq = np.where(index < HALF, index, index - SIZE)
    wave = freq * (2.0 * math.pi / SIZE)
    line = np.fft.ifft(np.exp(-0.5j * TIME_STEP * wave * wave))
    full = line[(index[:, None] - index[None, :]) % SIZE]
    left = []
    for sign in (1.0, -1.0):
        half = 0.5 * (full[:HALF, :HALF] + sign * full[:HALF, HALF:])
        real = np.block([[half.real, -half.imag], [half.imag, half.real]]).astype(np.float32)
        high = real.astype(ml_dtypes.bfloat16)
        low = (real - high.astype(np.float32)).astype(ml_dtypes.bfloat16)
        left.append(np.concatenate([high, high, low], axis=1))
    left = np.stack(left)
    return left, np.ascontiguousarray(np.swapaxes(left, 1, 2))


def cos_sin(angle):
    turns = jnp.floor(angle * (2.0 / math.pi) + 0.5)
    rest = angle - turns * 1.5703125
    rest = rest - turns * 4.837512969970703125e-4
    rest = rest - turns * 7.54978995489188216e-8
    square = rest * rest
    sine = ((-1.9515295891e-4 * square + 8.3321608736e-3) * square - 1.6666654611e-1) * square * rest + rest
    cosine = ((2.443315711809948e-5 * square - 1.388731625493765e-3) * square + 4.166664568298827e-2) * (
        square * square
    ) - 0.5 * square + 1.0
    quarter = turns.astype(jnp.int32)
    odd = (quarter & 1) == 1
    cos_out = jnp.where(odd, sine, cosine)
    sin_out = jnp.where(odd, cosine, sine)
    cos_out = jnp.where(((quarter + 1) & 2) == 2, -cos_out, cos_out)
    sin_out = jnp.where((quarter & 2) == 2, -sin_out, sin_out)
    return cos_out, sin_out


def split(values, axis):
    high = values.astype(jnp.bfloat16)
    low = (values - high.astype(jnp.float32)).astype(jnp.bfloat16)
    return jnp.concatenate([high, low, high], axis=axis)


def three_parts(values):
    high = values.astype(jnp.bfloat16)
    rest = values - high.astype(jnp.float32)
    middle = rest.astype(jnp.bfloat16)
    low = (rest - middle.astype(jnp.float32)).astype(jnp.bfloat16)
    return jnp.concatenate([high, middle, low], axis=0)


def dot(left, right):
    return jnp.dot(left, right, preferred_element_type=jnp.float32)


def propagate_rows(table, real, imag):
    plus = jnp.concatenate([real[:HALF] + real[HALF:], imag[:HALF] + imag[HALF:]], axis=0)
    minus = jnp.concatenate([real[:HALF] - real[HALF:], imag[:HALF] - imag[HALF:]], axis=0)
    plus = dot(table[0], split(plus, 0))
    minus = dot(table[1], split(minus, 0))
    low, high = plus + minus, plus - minus
    return (
        jnp.concatenate([low[:HALF], high[:HALF]], axis=0),
        jnp.concatenate([low[HALF:], high[HALF:]], axis=0),
    )


def propagate_lanes(table, real, imag):
    plus = jnp.concatenate([real[0] + real[1], imag[0] + imag[1]], axis=1)
    minus = jnp.concatenate([real[0] - real[1], imag[0] - imag[1]], axis=1)
    plus = dot(split(plus, 1), table[0])
    minus = dot(split(minus, 1), table[1])
    low, high = plus + minus, plus - minus
    return (
        jnp.concatenate([low[:, :HALF], high[:, :HALF]], axis=1),
        jnp.concatenate([low[:, HALF:], high[:, HALF:]], axis=1),
    )


def atom_matrix(atom_ref):
    atoms = lax.broadcasted_iota(jnp.int32, (ATOMS, ENTRIES), 0)
    return jnp.where(atoms == atom_ref[...], 1.0, 0.0).astype(jnp.bfloat16)


def project_kernel(
    block, count, atom_ref, slot_ref, orbs_hbm, potential_hbm, projectors_hbm, sent, masked_ref,
    orbs, potential, projectors, rows, counts, table, packed, sems,
):
    half_rows = PLANES * SIZE

    def load(source, into, sem):
        return [
            pltpu.make_async_copy(
                source.at[:, pl.ds(z * LANES, LANES)], into.at[pl.ds(z * half_rows, half_rows)], sem.at[z]
            )
            for z in range(2)
        ]

    copies = [load(potential_hbm, potential, sems.at[4])]
    copies += [load(orbs_hbm.at[k], orbs.at[k], sems.at[k]) for k in range(4)]
    projectors_copy = pltpu.make_async_copy(projectors_hbm, projectors, sems.at[5, 0])
    for pair in copies:
        for copy in pair:
            copy.start()
    projectors_copy.start()

    def arrived(pair):
        for copy in pair:
            copy.wait()

    def place(entry):
        at = block[entry]
        return (at & 1) * half_rows + lax.shift_right_logical(at, 1)

    arrived(copies[0])

    def first(entry, carry):
        rows[4, pl.ds(entry, 1), :] = potential[pl.ds(place(entry), 1), :]
        counts[pl.ds(entry, 1), :] = jnp.full((1, LANES), count[entry], jnp.int32)
        return carry

    lax.fori_loop(0, ENTRIES, first, 0, unroll=32)
    cosine, sine = cos_sin((0.5 * TIME_STEP) * rows[4])
    rows[4] = cosine
    rows[5] = sine
    for k in range(4):
        arrived(copies[k + 1])

        def step(entry, carry):
            rows[k, pl.ds(entry, 1), :] = orbs[k, pl.ds(place(entry), 1), :]
            return carry

        lax.fori_loop(0, ENTRIES, step, 0, unroll=32)

    projectors_copy.wait()
    piece = 64

    def reduce(index, carry):
        at = pl.ds(pl.multiple_of(index * piece, piece), piece)
        lane = lax.broadcasted_iota(jnp.int32, (piece, LANES), 1)
        cosine, sine = rows[4, at, :], rows[5, at, :]
        inside = lane < counts[at, :]
        fields = []
        for n in range(ORBS):
            real, imag = rows[n, at, :], rows[ORBS + n, at, :]
            fields += [(n, cosine * real + sine * imag), (ORBS + n, cosine * imag - sine * real)]
        out = jnp.zeros((piece, LANES), jnp.float32)
        for f in range(4):
            masked = jnp.where(inside, projectors[f, at, :], 0.0)
            if f == 0:
                masked_ref[at, :] = masked
            for k, field in fields:
                total = jnp.sum(masked * field, axis=1, keepdims=True)
                out = jnp.where(lane == f * 4 + k, total, out)
        table[at, :] = out
        return carry

    lax.fori_loop(0, ENTRIES // piece, reduce, 0)
    turned = jnp.transpose(table[...])[:16]
    sums = lax.dot_general(
        three_parts(turned), atom_matrix(atom_ref), (((1,), (1,)), ((), ())), preferred_element_type=jnp.float32
    )
    sums = sums[:16] + sums[16:32] + sums[32:]
    for k in range(4):
        for q in range(4):
            packed[k * 4 + q : k * 4 + q + 1, :] = sums[k : k + 1, q * LANES : (q + 1) * LANES]
    slots = lax.dot_general(
        three_parts(sums), atom_matrix(slot_ref), (((1,), (1,)), ((), ())), preferred_element_type=jnp.float32
    )
    slots = slots[:16] + slots[16:32] + slots[32:]
    lane = lax.broadcasted_iota(jnp.int32, (8, LANES), 1)
    for d in range(GROUPS):
        tile = slots[:, d // 8 * LANES : (d // 8 + 1) * LANES]
        begin = d % 8 * OWNED
        upper = pltpu.roll(tile[:8], (LANES - begin) % LANES, 1)
        lower = pltpu.roll(tile[8:], (LANES - begin + OWNED) % LANES, 1)
        sent[d, 0:16, :] = packed[...]
        sent[d, 16:24, :] = jnp.where(lane < OWNED, upper, lower)


def project(orbs, potential, projectors, entry_atom, entry_block, entry_count, owner_slot):
    smem = pl.BlockSpec(memory_space=pltpu.SMEM)
    vmem = pl.BlockSpec(memory_space=pltpu.VMEM)
    hbm = pl.BlockSpec(memory_space=pltpu.HBM)
    rows = PLANES * SIZE
    return pl.pallas_call(
        project_kernel,
        out_shape=(
            jax.ShapeDtypeStruct((GROUPS, SENT, LANES), jnp.float32),
            jax.ShapeDtypeStruct((ENTRIES, LANES), jnp.float32),
        ),
        in_specs=[smem, smem, vmem, vmem, hbm, hbm, hbm],
        out_specs=(vmem, vmem),
        scratch_shapes=[
            pltpu.VMEM((4, 2 * rows, LANES), jnp.float32),
            pltpu.VMEM((2 * rows, LANES), jnp.float32),
            pltpu.VMEM((4, ENTRIES, LANES), jnp.float32),
            pltpu.VMEM((6, ENTRIES, LANES), jnp.float32),
            pltpu.VMEM((ENTRIES, LANES), jnp.int32),
            pltpu.VMEM((ENTRIES, LANES), jnp.float32),
            pltpu.VMEM((16, LANES), jnp.float32),
            pltpu.SemaphoreType.DMA((6, 2)),
        ],
        compiler_params=pltpu.CompilerParams(vmem_limit_bytes=VMEM),
        cost_estimate=pl.CostEstimate(flops=10**9, bytes_accessed=36 * 10**6, transcendentals=0),
        name="project",
    )(
        entry_block, entry_count, entry_atom.reshape(1, ENTRIES), owner_slot.reshape(1, ATOMS), orbs, potential, projectors
    )


SHIFT_STEP = 8


def shift_kernel(orbs, potential, *rest):
    out = rest[-1]
    for x in range(PLANES):
        cosine, sine = cos_sin((0.5 * TIME_STEP) * potential[x])
        real, imag = orbs[0, 0, x], orbs[1, 0, x]
        both = (cosine * real + sine * imag, cosine * imag - sine * real)
        for c in range(2):
            for d in range(SHIFT_STEP):
                for z in range(2):
                    tile = both[c][d * 8 : d * 8 + 8, z * LANES : (z + 1) * LANES]
                    out[pl.ds(d * 256 + c * 16 + z * 8 + x, 8, stride=32), :] = tile


def shift(n, orbitals, potential, *first):
    width = SHIFT_STEP * 8
    return pl.pallas_call(
        shift_kernel,
        grid=(GROUPS // SHIFT_STEP,),
        out_shape=pltpu.HBM((GROUPS * 256, LANES), jnp.float32),
        in_specs=[
            pl.BlockSpec((2, 1, PLANES, width, SIZE), lambda i: (0, n, 0, i, 0)),
            pl.BlockSpec((PLANES, width, SIZE), lambda i: (0, i, 0)),
            *[pl.BlockSpec(memory_space=pl.ANY) for _ in first],
        ],
        out_specs=pl.BlockSpec((SHIFT_STEP * 256, LANES), lambda i: (i, 0)),
        compiler_params=pltpu.CompilerParams(vmem_limit_bytes=VMEM),
        cost_estimate=pl.CostEstimate(flops=10**8, bytes_accessed=11 * 10**6, transcendentals=0),
        name=f"shift{n}",
    )(orbitals, potential, *first)


def correct_kernel(n, place, received, strength, atom_ref, masked, right, before, after, field, coefs, updates, sems):
    load = pltpu.make_async_copy(before, field, sems.at[0])
    load.start()
    sums = jnp.sum(received[:, 0:16, :], axis=0)
    real = sums[n * 4 : n * 4 + 4]
    imag = sums[(ORBS + n) * 4 : (ORBS + n) * 4 + 4]
    cosine, sine = cos_sin(TIME_STEP * strength[...])
    less_one = cosine - 1.0
    both = (less_one * real + sine * imag, less_one * imag - sine * real)
    coefs[...] = jnp.zeros_like(coefs)
    for c in range(2):
        for q in range(4):
            coefs[c : c + 1, q * LANES : (q + 1) * LANES] = both[c][q : q + 1]
    spread = dot(three_parts(coefs[...]), atom_matrix(atom_ref))
    spread = jnp.transpose(spread[:16] + spread[16:32] + spread[32:])
    for c in range(2):
        updates[c] = spread[:, c : c + 1] * masked[...]
    load.wait()

    def step(entry, carry):
        row = place[entry]
        at = [pl.ds(row + c * 16, 1) for c in range(2)]
        both = [field[at[c], :] + updates[c, pl.ds(entry, 1), :] for c in range(2)]
        for c in range(2):
            field[at[c], :] = both[c]
        return carry

    lax.fori_loop(0, ENTRIES, step, 0, unroll=32)
    if n in EARLY:
        tiles = field.reshape(GROUPS * 8, 2, 2, 8, LANES)

        def z_lines(index, carry):
            at = pl.ds(index * 32, 32)
            real, imag = ([tiles[at, c, z].reshape(SIZE, LANES) for z in range(2)] for c in range(2))
            both = propagate_lanes(right, real, imag)
            for c in range(2):
                for z in range(2):
                    tiles[at, c, z] = both[c][:, z * LANES : (z + 1) * LANES].reshape(32, 8, LANES)
            return carry

        lax.fori_loop(0, GROUPS * 8 // 32, z_lines, 0)
    store = pltpu.make_async_copy(field, after, sems.at[1])
    store.start()
    store.wait()


def correct(n, place, received, strength, atoms, masked, right, before):
    smem = pl.BlockSpec(memory_space=pltpu.SMEM)
    vmem = pl.BlockSpec(memory_space=pltpu.VMEM)
    hbm = pl.BlockSpec(memory_space=pltpu.HBM)
    return pl.pallas_call(
        functools.partial(correct_kernel, n),
        out_shape=pltpu.HBM((GROUPS * 256, LANES), jnp.float32),
        in_specs=[smem, vmem, vmem, vmem, vmem, vmem, hbm],
        out_specs=hbm,
        scratch_shapes=[
            pltpu.VMEM((GROUPS * 256, LANES), jnp.float32),
            pltpu.VMEM((16, ATOMS), jnp.float32),
            pltpu.VMEM((2, ENTRIES, LANES), jnp.float32),
            pltpu.SemaphoreType.DMA((2,)),
        ],
        input_output_aliases={6: 0},
        compiler_params=pltpu.CompilerParams(vmem_limit_bytes=24 << 20),
        cost_estimate=pl.CostEstimate(flops=5 * 10**8, bytes_accessed=20 * 10**6, transcendentals=0),
        name=f"correct{n}",
    )(place, received, strength, atoms, masked, right if n in EARLY else right[:, :8, :LANES], before)


LINES_STEP = 4


def lines_kernel(n, field, left, right, *rest):
    *chunks, half_done, turned, sems = rest[-3 - len(CHUNKS) :]
    step = pl.program_id(0)
    last = step == pl.num_programs(0) - 1
    rows = turned.reshape(GROUPS, 2, PLANES * 16, LANES)

    def x_lines(z, y, real, imag):
        both = propagate_rows(left, jnp.concatenate(real, axis=1), jnp.concatenate(imag, axis=1))
        for c in range(2):
            for k in range(2):
                for d in range(GROUPS):
                    tile = both[c][d * 8 : d * 8 + 8, k * LANES : (k + 1) * LANES]
                    rows[d, z, pl.ds(c * 8 + y + k, 8, stride=16), :] = tile

    def copies(z):
        begin = 0
        for k, (chunk, planes) in enumerate(zip(chunks, CHUNKS)):
            part = turned.at[:, z, pl.ds(begin, planes)]
            yield pltpu.make_async_copy(part, chunk.at[:, :, n, z], sems.at[z, k])
            begin += planes

    if n in EARLY:
        for z in range(2):
            for k in range(0, LINES_STEP, 2):
                parts = ([field[:, k + j, c, z].reshape(SIZE, LANES) for j in range(2)] for c in range(2))
                x_lines(z, step * LINES_STEP + k, *parts)

            @pl.when(last)
            def _():
                for copy in copies(z):
                    copy.start()

    else:
        for k in range(LINES_STEP):
            real, imag = ([field[:, k, c, z].reshape(SIZE, LANES) for z in range(2)] for c in range(2))
            both = propagate_lanes(right, real, imag)
            y = step * LINES_STEP + k
            for c in range(2):
                for z in range(2):
                    half_done[c, z, y] = both[c][:, z * LANES : (z + 1) * LANES]

        @pl.when(last)
        def _():
            for z in range(2):
                for y in range(0, 8, 2):
                    x_lines(z, y, *([half_done[c, z, y + j] for j in range(2)] for c in range(2)))
                for copy in copies(z):
                    copy.start()

    @pl.when(last)
    def _():
        for z in range(2):
            for copy in copies(z):
                copy.wait()


def lines(n, field, left, right, before=(), first=()):
    hbm = pl.BlockSpec(memory_space=pltpu.HBM)
    return pl.pallas_call(
        functools.partial(lines_kernel, n),
        grid=(8 // LINES_STEP,),
        out_shape=tuple(
            jax.ShapeDtypeStruct((GROUPS, planes, ORBS, 2, 16, LANES), jnp.float32) for planes in CHUNKS
        ),
        in_specs=[
            pl.BlockSpec((GROUPS, LINES_STEP, 2, 2, 8, LANES), lambda i: (0, i, 0, 0, 0, 0)),
            pl.BlockSpec(left.shape, lambda i: (0, 0, 0)),
            pl.BlockSpec(right.shape, lambda i: (0, 0, 0)),
            *[hbm for _ in (*before, *first)],
        ],
        out_specs=tuple(hbm for _ in CHUNKS),
        scratch_shapes=[
            pltpu.VMEM((2, 2, 8, SIZE, LANES), jnp.float32),
            pltpu.VMEM((GROUPS, 2, PLANES, 16, LANES), jnp.float32),
            pltpu.SemaphoreType.DMA((2, len(CHUNKS))),
        ],
        input_output_aliases={3 + k: k for k in range(len(before))},
        compiler_params=pltpu.CompilerParams(vmem_limit_bytes=VMEM),
        cost_estimate=pl.CostEstimate(flops=5 * 10**9, bytes_accessed=10 * 10**6, transcendentals=0),
        name=f"lines{n}",
    )(field.reshape(GROUPS, 8, 2, 2, 8, LANES), left, right, *before, *first)


def finish_kernel(halves, band, field, potential, left, *rest):
    out, *pieces, whole = rest[-2 - BANDS * halves :]
    cosine, sine = cos_sin((0.5 * TIME_STEP) * potential[0])
    total = None
    for n in range(ORBS):
        real, imag = (
            jnp.concatenate([field[:, 0, n, z, c].reshape(SIZE, LANES) for z in range(2)], axis=1) for c in range(2)
        )
        real, imag = propagate_rows(left, real, imag)
        real, imag = cosine * real + sine * imag, cosine * imag - sine * real
        out[0, n, 0] = real
        out[1, n, 0] = imag
        square = real * real + imag * imag
        total = square if total is None else total + square
    whole[...] = total
    rows = SIZE // BANDS // halves
    for k, piece in enumerate(pieces):
        begin = (band[0] + k // halves) % BANDS * halves + k % halves
        piece[0] = whole[pl.ds(pl.multiple_of(begin * rows, rows), rows), :]


def finish(planes, begin, halves, band, field, potential, left, before=(), first=()):
    rows = SIZE // BANDS // halves
    return pl.pallas_call(
        functools.partial(finish_kernel, halves),
        grid=(planes,),
        out_shape=(
            jax.ShapeDtypeStruct((2, ORBS, PLANES, SIZE, SIZE), jnp.float32),
            *[jax.ShapeDtypeStruct((planes, rows, SIZE), jnp.float32) for _ in range(BANDS * halves)],
        ),
        in_specs=[
            pl.BlockSpec(memory_space=pltpu.SMEM),
            pl.BlockSpec((GROUPS, 1, ORBS, 2, 2, 8, LANES), lambda i: (0, i, 0, 0, 0, 0, 0)),
            pl.BlockSpec((1, SIZE, SIZE), lambda i: (i + begin, 0, 0)),
            pl.BlockSpec(left.shape, lambda i: (0, 0, 0)),
            *[pl.BlockSpec(memory_space=pl.ANY) for _ in (*before, *first)],
        ],
        out_specs=(
            pl.BlockSpec((2, ORBS, 1, SIZE, SIZE), lambda i: (0, 0, i + begin, 0, 0)),
            *[pl.BlockSpec((1, rows, SIZE), lambda i: (i, 0, 0)) for _ in range(BANDS * halves)],
        ),
        scratch_shapes=[pltpu.VMEM((SIZE, SIZE), jnp.float32)],
        input_output_aliases={4 + k: k for k in range(len(before))},
        compiler_params=pltpu.CompilerParams(vmem_limit_bytes=VMEM),
        cost_estimate=pl.CostEstimate(flops=10**9 * planes, bytes_accessed=3 * 10**6 * planes, transcendentals=0),
        name=f"finish{begin}",
    )(band, field.reshape(GROUPS, planes, ORBS, 2, 2, 8, LANES), potential, left, *before, *first)


def collect_kernel(owners, band, *refs):
    out, mark = refs[-2:]
    mark[...] = jnp.zeros_like(mark)
    rows = SIZE // BANDS
    for piece, (owner, offset) in zip(refs, owners):
        row = pl.multiple_of((band[0] + owner) % BANDS * rows, rows)
        out[0, pl.ds(pl.multiple_of(row + offset, rows // 2), piece.shape[1]), :] = piece[0]


def collect(begin, band, pieces, owners, *before):
    return pl.pallas_call(
        functools.partial(collect_kernel, owners),
        grid=(pieces[0].shape[0],),
        out_shape=(
            jax.ShapeDtypeStruct((PLANES, SIZE, SIZE), jnp.float32),
            jax.ShapeDtypeStruct((8, LANES), jnp.float32),
        ),
        in_specs=[
            pl.BlockSpec(memory_space=pltpu.SMEM),
            *[pl.BlockSpec((1, piece.shape[1], SIZE), lambda i: (i, 0, 0)) for piece in pieces],
            *[pl.BlockSpec(memory_space=pltpu.HBM) for _ in before],
        ],
        out_specs=(
            pl.BlockSpec((1, SIZE, SIZE), lambda i: (i + begin, 0, 0)),
            pl.BlockSpec((8, LANES), lambda i: (0, 0)),
        ),
        input_output_aliases={1 + len(pieces) + k: k for k in range(len(before))},
        compiler_params=pltpu.CompilerParams(vmem_limit_bytes=VMEM if begin == 0 else 16 << 20),
        cost_estimate=pl.CostEstimate(flops=0, bytes_accessed=3 * 10**6, transcendentals=0),
        name=f"collect{begin}",
    )(band, *pieces, *before)


def onward(array, steps):
    return lax.ppermute(array, "band", [(b, (b + steps) % BANDS) for b in range(BANDS)])


def ring_reduce(pieces):
    own_low, own_high, next_low, next_high, across_low, across_high, last_low, last_high = pieces
    from_last = onward(across_low, 1)
    from_next = onward(across_high, 3)
    high = own_high + onward(next_high, 1)
    low = own_low + onward(last_low, 3)
    return low + onward(next_low + from_last, 1), high + onward(last_high + from_next, 3)


def ring_gather(low, high):
    last_low, next_high = onward(low, 1), onward(high, 3)
    last_high, next_low = onward(high, 1), onward(low, 3)
    pieces = low, high, last_low, last_high, next_low, next_high, onward(last_low, 1), onward(next_high, 3)
    half = SIZE // BANDS // 2
    return pieces, tuple((owner, offset) for owner in (0, 3, 1, 2) for offset in (0, half))


def add_kernel(own, from_last, across, from_next, *rest):
    rest[-1][...] = own[...] + from_last[...] + across[...] + from_next[...]


def direct_reduce(pieces, first):
    parts = [pieces[0], *[onward(pieces[k], k) for k in range(1, BANDS)]]
    return pl.pallas_call(
        add_kernel,
        out_shape=jax.ShapeDtypeStruct(pieces[0].shape, jnp.float32),
        in_specs=[
            *[pl.BlockSpec(memory_space=pltpu.VMEM) for _ in parts],
            *[pl.BlockSpec(memory_space=pltpu.HBM) for _ in first],
        ],
        out_specs=pl.BlockSpec(memory_space=pltpu.VMEM),
        compiler_params=pltpu.CompilerParams(vmem_limit_bytes=16 << 20),
        cost_estimate=pl.CostEstimate(flops=10**6, bytes_accessed=10**6, transcendentals=0),
        name="add",
    )(*parts, *first)


def direct_gather(total):
    return (total, *[onward(total, k) for k in range(1, BANDS)]), ((0, 0), (3, 0), (2, 0), (1, 0))


def exchange(array):
    return lax.all_to_all(array, "grid", split_axis=0, concat_axis=0, tiled=True)


def body(left, right, orbitals, potential, projectors, entry_atom, entry_block, entry_count, owner_slot, strength):
    atom_ids = jnp.arange(ATOMS, dtype=jnp.int32)
    rows = PLANES * SIZE
    band = lax.axis_index("band").astype(jnp.int32).reshape(1)
    sent, masked = project(
        orbitals.reshape(2 * ORBS, rows, SIZE), potential.reshape(rows, SIZE), projectors,
        entry_atom, entry_block, entry_count, owner_slot,
    )
    received = exchange(sent)
    x, y, z = entry_block // 512, (entry_block // 2) % SIZE, entry_block % 2
    place = y * 32 + z * 8 + x
    in_slot = owner_slot[:, None] == atom_ids[None, :]
    strength_atom = jnp.sum(jnp.where(in_slot, strength[None, :], 0.0), axis=1).reshape(4, LANES)
    atoms = entry_atom.reshape(1, ENTRIES)
    pencils, sent = [], ()
    for n in range(ORBS):
        shifted = shift(n, orbitals, potential, *sent)
        fixed = correct(n, place, received, strength_atom, atoms, masked, right, shifted)
        pencils.append(exchange(fixed.reshape(GROUPS, 256, LANES)))
        sent = (fixed,)
    mine = jnp.sum(received[:, 16:], axis=0)
    mine = jnp.concatenate([mine[:, :OWNED], mine[:, OWNED : 2 * OWNED]], axis=0).reshape(4, 2 * ORBS, OWNED)
    strength_mine = lax.dynamic_slice_in_dim(strength, lax.axis_index("grid") * OWNED, OWNED)
    forces = -2.0 * strength_mine * jnp.sum(mine[0][None] * mine[1:], axis=1)
    forces = sum([onward(forces, k) for k in range(1, BANDS)], forces)

    back = lines(0, pencils[0], left, right)
    back = lines(1, pencils[1], left, right, back, (forces,))
    out, density, ready, marks, begin = (), (), (), (), 0
    for k, planes in enumerate(CHUNKS):
        field = exchange(back[k])
        made, *pieces = finish(planes, begin, 2 if k == 0 else 1, band, field, potential, left, out, ready)
        out = (made,)
        if k == 0:
            sums, owners = ring_gather(*ring_reduce(pieces))
            ready = sums[2:]
        else:
            sums, owners = direct_gather(direct_reduce(pieces, marks))
        made, mark = collect(begin, band, sums, owners, *density)
        density, marks = (made,), (mark,)
        begin += planes
    return out[0], density[0], forces


def solution(mesh):
    left, right = propagator_tables()
    in_specs = (
        P(None, "band", "grid", None, None),
        P("grid", None, None),
        P(None, "grid", None),
        P("grid"),
        P("grid"),
        P("grid"),
        P(),
        P(),
    )
    out_specs = (P(None, "band", "grid", None, None), P("grid", None, None), P(None, "grid"))

    def run(*args):
        return body(jnp.asarray(left), jnp.asarray(right), *args)

    return jax.shard_map(run, mesh=mesh, in_specs=in_specs, out_specs=out_specs, check_vma=False)
```

```python
import functools
import math

import jax
import jax.numpy as jnp
import ml_dtypes
import numpy as np
from jax import lax
from jax.experimental import pallas as pl
from jax.experimental.pallas import tpu as pltpu
from jax.sharding import PartitionSpec as P

SIZE = 256
HALF = SIZE // 2
LANES = 128
TIME_STEP = 4.0
HIGHEST = lax.Precision.HIGHEST
ORBS = 2
EARLY = (1,)
BANDS = 4
PLANES = 8
GROUPS = 32
ENTRIES = 512
ATOMS = 512
OWNED = ATOMS // GROUPS
CHUNKS = (5, 3)
VMEM = 56 << 20
SENT = 24


def propagator_tables():
    index = np.arange(SIZE)
    freq = np.where(index < HALF, index, index - SIZE)
    wave = freq * (2.0 * math.pi / SIZE)
    line = np.fft.ifft(np.exp(-0.5j * TIME_STEP * wave * wave))
    full = line[(index[:, None] - index[None, :]) % SIZE]
    left = []
    for sign in (1.0, -1.0):
        half = 0.5 * (full[:HALF, :HALF] + sign * full[:HALF, HALF:])
        real = np.block([[half.real, -half.imag], [half.imag, half.real]]).astype(np.float32)
        high = real.astype(ml_dtypes.bfloat16)
        low = (real - high.astype(np.float32)).astype(ml_dtypes.bfloat16)
        left.append(np.concatenate([high, high, low], axis=1))
    left = np.stack(left)
    return left, np.ascontiguousarray(np.swapaxes(left, 1, 2))


def cos_sin(angle):
    turns = jnp.floor(angle * (2.0 / math.pi) + 0.5)
    rest = angle - turns * 1.5703125
    rest = rest - turns * 4.837512969970703125e-4
    rest = rest - turns * 7.54978995489188216e-8
    square = rest * rest
    sine = ((-1.9515295891e-4 * square + 8.3321608736e-3) * square - 1.6666654611e-1) * square * rest + rest
    cosine = ((2.443315711809948e-5 * square - 1.388731625493765e-3) * square + 4.166664568298827e-2) * (
        square * square
    ) - 0.5 * square + 1.0
    quarter = turns.astype(jnp.int32)
    odd = (quarter & 1) == 1
    cos_out = jnp.where(odd, sine, cosine)
    sin_out = jnp.where(odd, cosine, sine)
    cos_out = jnp.where(((quarter + 1) & 2) == 2, -cos_out, cos_out)
    sin_out = jnp.where((quarter & 2) == 2, -sin_out, sin_out)
    return cos_out, sin_out


def split(values, axis):
    high = values.astype(jnp.bfloat16)
    low = (values - high.astype(jnp.float32)).astype(jnp.bfloat16)
    return jnp.concatenate([high, low, high], axis=axis)


def three_parts(values):
    high = values.astype(jnp.bfloat16)
    rest = values - high.astype(jnp.float32)
    middle = rest.astype(jnp.bfloat16)
    low = (rest - middle.astype(jnp.float32)).astype(jnp.bfloat16)
    return jnp.concatenate([high, middle, low], axis=0)


def dot(left, right):
    return jnp.dot(left, right, preferred_element_type=jnp.float32)


def propagate_rows(table, real, imag):
    plus = jnp.concatenate([real[:HALF] + real[HALF:], imag[:HALF] + imag[HALF:]], axis=0)
    minus = jnp.concatenate([real[:HALF] - real[HALF:], imag[:HALF] - imag[HALF:]], axis=0)
    plus = dot(table[0], split(plus, 0))
    minus = dot(table[1], split(minus, 0))
    low, high = plus + minus, plus - minus
    return (
        jnp.concatenate([low[:HALF], high[:HALF]], axis=0),
        jnp.concatenate([low[HALF:], high[HALF:]], axis=0),
    )


def propagate_lanes(table, real, imag):
    plus = jnp.concatenate([real[0] + real[1], imag[0] + imag[1]], axis=1)
    minus = jnp.concatenate([real[0] - real[1], imag[0] - imag[1]], axis=1)
    plus = dot(split(plus, 1), table[0])
    minus = dot(split(minus, 1), table[1])
    low, high = plus + minus, plus - minus
    return (
        jnp.concatenate([low[:, :HALF], high[:, :HALF]], axis=1),
        jnp.concatenate([low[:, HALF:], high[:, HALF:]], axis=1),
    )


def atom_matrix(atom_ref):
    atoms = lax.broadcasted_iota(jnp.int32, (ATOMS, ENTRIES), 0)
    return jnp.where(atoms == atom_ref[...], 1.0, 0.0).astype(jnp.bfloat16)


def project_kernel(
    block, count, atom_ref, slot_ref, orbs_hbm, potential_hbm, projectors_hbm, sent, masked_ref,
    orbs, potential, projectors, rows, counts, table, packed, sems,
):
    half_rows = PLANES * SIZE

    def load(source, into, sem):
        return [
            pltpu.make_async_copy(
                source.at[:, pl.ds(z * LANES, LANES)], into.at[pl.ds(z * half_rows, half_rows)], sem.at[z]
            )
            for z in range(2)
        ]

    copies = [load(potential_hbm, potential, sems.at[4])]
    copies += [load(orbs_hbm.at[k], orbs.at[k], sems.at[k]) for k in range(4)]
    projectors_copy = pltpu.make_async_copy(projectors_hbm, projectors, sems.at[5, 0])
    for pair in copies:
        for copy in pair:
            copy.start()
    projectors_copy.start()

    def arrived(pair):
        for copy in pair:
            copy.wait()

    def place(entry):
        at = block[entry]
        return (at & 1) * half_rows + lax.shift_right_logical(at, 1)

    arrived(copies[0])

    def first(entry, carry):
        rows[4, pl.ds(entry, 1), :] = potential[pl.ds(place(entry), 1), :]
        counts[pl.ds(entry, 1), :] = jnp.full((1, LANES), count[entry], jnp.int32)
        return carry

    lax.fori_loop(0, ENTRIES, first, 0, unroll=32)
    cosine, sine = cos_sin((0.5 * TIME_STEP) * rows[4])
    rows[4] = cosine
    rows[5] = sine
    for k in range(4):
        arrived(copies[k + 1])

        def step(entry, carry):
            rows[k, pl.ds(entry, 1), :] = orbs[k, pl.ds(place(entry), 1), :]
            return carry

        lax.fori_loop(0, ENTRIES, step, 0, unroll=32)

    projectors_copy.wait()
    piece = 64

    def reduce(index, carry):
        at = pl.ds(pl.multiple_of(index * piece, piece), piece)
        lane = lax.broadcasted_iota(jnp.int32, (piece, LANES), 1)
        cosine, sine = rows[4, at, :], rows[5, at, :]
        inside = lane < counts[at, :]
        fields = []
        for n in range(ORBS):
            real, imag = rows[n, at, :], rows[ORBS + n, at, :]
            fields += [(n, cosine * real + sine * imag), (ORBS + n, cosine * imag - sine * real)]
        out = jnp.zeros((piece, LANES), jnp.float32)
        for f in range(4):
            masked = jnp.where(inside, projectors[f, at, :], 0.0)
            if f == 0:
                masked_ref[at, :] = masked
            for k, field in fields:
                total = jnp.sum(masked * field, axis=1, keepdims=True)
                out = jnp.where(lane == f * 4 + k, total, out)
        table[at, :] = out
        return carry

    lax.fori_loop(0, ENTRIES // piece, reduce, 0, unroll=2)
    turned = jnp.transpose(table[...])[:16]
    sums = lax.dot_general(
        three_parts(turned), atom_matrix(atom_ref), (((1,), (1,)), ((), ())), preferred_element_type=jnp.float32
    )
    sums = sums[:16] + sums[16:32] + sums[32:]
    for k in range(4):
        for q in range(4):
            packed[k * 4 + q : k * 4 + q + 1, :] = sums[k : k + 1, q * LANES : (q + 1) * LANES]
    slots = lax.dot_general(
        three_parts(sums), atom_matrix(slot_ref), (((1,), (1,)), ((), ())), preferred_element_type=jnp.float32
    )
    slots = slots[:16] + slots[16:32] + slots[32:]
    lane = lax.broadcasted_iota(jnp.int32, (8, LANES), 1)
    for d in range(GROUPS):
        tile = slots[:, d // 8 * LANES : (d // 8 + 1) * LANES]
        begin = d % 8 * OWNED
        upper = pltpu.roll(tile[:8], (LANES - begin) % LANES, 1)
        lower = pltpu.roll(tile[8:], (LANES - begin + OWNED) % LANES, 1)
        sent[d, 0:16, :] = packed[...]
        sent[d, 16:24, :] = jnp.where(lane < OWNED, upper, lower)


def project(orbs, potential, projectors, entry_atom, entry_block, entry_count, owner_slot):
    smem = pl.BlockSpec(memory_space=pltpu.SMEM)
    vmem = pl.BlockSpec(memory_space=pltpu.VMEM)
    hbm = pl.BlockSpec(memory_space=pltpu.HBM)
    rows = PLANES * SIZE
    return pl.pallas_call(
        project_kernel,
        out_shape=(
            jax.ShapeDtypeStruct((GROUPS, SENT, LANES), jnp.float32),
            jax.ShapeDtypeStruct((ENTRIES, LANES), jnp.float32),
        ),
        in_specs=[smem, smem, vmem, vmem, hbm, hbm, hbm],
        out_specs=(vmem, vmem),
        scratch_shapes=[
            pltpu.VMEM((4, 2 * rows, LANES), jnp.float32),
            pltpu.VMEM((2 * rows, LANES), jnp.float32),
            pltpu.VMEM((4, ENTRIES, LANES), jnp.float32),
            pltpu.VMEM((6, ENTRIES, LANES), jnp.float32),
            pltpu.VMEM((ENTRIES, LANES), jnp.int32),
            pltpu.VMEM((ENTRIES, LANES), jnp.float32),
            pltpu.VMEM((16, LANES), jnp.float32),
            pltpu.SemaphoreType.DMA((6, 2)),
        ],
        compiler_params=pltpu.CompilerParams(vmem_limit_bytes=VMEM),
        cost_estimate=pl.CostEstimate(flops=10**9, bytes_accessed=36 * 10**6, transcendentals=0),
        name="project",
    )(
        entry_block, entry_count, entry_atom.reshape(1, ENTRIES), owner_slot.reshape(1, ATOMS), orbs, potential, projectors
    )


SHIFT_STEP = 8


def shift_kernel(orbs, potential, *rest):
    out = rest[-1]
    for x in range(PLANES):
        cosine, sine = cos_sin((0.5 * TIME_STEP) * potential[x])
        real, imag = orbs[0, 0, x], orbs[1, 0, x]
        both = (cosine * real + sine * imag, cosine * imag - sine * real)
        for c in range(2):
            for d in range(SHIFT_STEP):
                for z in range(2):
                    tile = both[c][d * 8 : d * 8 + 8, z * LANES : (z + 1) * LANES]
                    out[pl.ds(d * 256 + c * 16 + z * 8 + x, 8, stride=32), :] = tile


def shift(n, orbitals, potential, *first):
    width = SHIFT_STEP * 8
    return pl.pallas_call(
        shift_kernel,
        grid=(GROUPS // SHIFT_STEP,),
        out_shape=pltpu.HBM((GROUPS * 256, LANES), jnp.float32),
        in_specs=[
            pl.BlockSpec((2, 1, PLANES, width, SIZE), lambda i: (0, n, 0, i, 0)),
            pl.BlockSpec((PLANES, width, SIZE), lambda i: (0, i, 0)),
            *[pl.BlockSpec(memory_space=pl.ANY) for _ in first],
        ],
        out_specs=pl.BlockSpec((SHIFT_STEP * 256, LANES), lambda i: (i, 0)),
        compiler_params=pltpu.CompilerParams(vmem_limit_bytes=VMEM),
        cost_estimate=pl.CostEstimate(flops=10**8, bytes_accessed=11 * 10**6, transcendentals=0),
        name=f"shift{n}",
    )(orbitals, potential, *first)


def correct_kernel(n, place, received, strength, atom_ref, masked, right, before, after, field, coefs, updates, sems):
    load = pltpu.make_async_copy(before, field, sems.at[0])
    load.start()
    sums = jnp.sum(received[:, 0:16, :], axis=0)
    real = sums[n * 4 : n * 4 + 4]
    imag = sums[(ORBS + n) * 4 : (ORBS + n) * 4 + 4]
    cosine, sine = cos_sin(TIME_STEP * strength[...])
    less_one = cosine - 1.0
    both = (less_one * real + sine * imag, less_one * imag - sine * real)
    coefs[...] = jnp.zeros_like(coefs)
    for c in range(2):
        for q in range(4):
            coefs[c : c + 1, q * LANES : (q + 1) * LANES] = both[c][q : q + 1]
    spread = dot(three_parts(coefs[...]), atom_matrix(atom_ref))
    spread = jnp.transpose(spread[:16] + spread[16:32] + spread[32:])
    for c in range(2):
        updates[c] = spread[:, c : c + 1] * masked[...]
    load.wait()

    def step(entry, carry):
        row = place[entry]
        at = [pl.ds(row + c * 16, 1) for c in range(2)]
        both = [field[at[c], :] + updates[c, pl.ds(entry, 1), :] for c in range(2)]
        for c in range(2):
            field[at[c], :] = both[c]
        return carry

    lax.fori_loop(0, ENTRIES, step, 0, unroll=32)
    if n in EARLY:
        tiles = field.reshape(GROUPS * 8, 2, 2, 8, LANES)

        def z_lines(index, carry):
            at = pl.ds(index * 32, 32)
            real, imag = ([tiles[at, c, z].reshape(SIZE, LANES) for z in range(2)] for c in range(2))
            both = propagate_lanes(right, real, imag)
            for c in range(2):
                for z in range(2):
                    tiles[at, c, z] = both[c][:, z * LANES : (z + 1) * LANES].reshape(32, 8, LANES)
            return carry

        lax.fori_loop(0, GROUPS * 8 // 32, z_lines, 0)
    store = pltpu.make_async_copy(field, after, sems.at[1])
    store.start()
    store.wait()


def correct(n, place, received, strength, atoms, masked, right, before):
    smem = pl.BlockSpec(memory_space=pltpu.SMEM)
    vmem = pl.BlockSpec(memory_space=pltpu.VMEM)
    hbm = pl.BlockSpec(memory_space=pltpu.HBM)
    return pl.pallas_call(
        functools.partial(correct_kernel, n),
        out_shape=pltpu.HBM((GROUPS * 256, LANES), jnp.float32),
        in_specs=[smem, vmem, vmem, vmem, vmem, vmem, hbm],
        out_specs=hbm,
        scratch_shapes=[
            pltpu.VMEM((GROUPS * 256, LANES), jnp.float32),
            pltpu.VMEM((16, ATOMS), jnp.float32),
            pltpu.VMEM((2, ENTRIES, LANES), jnp.float32),
            pltpu.SemaphoreType.DMA((2,)),
        ],
        input_output_aliases={6: 0},
        compiler_params=pltpu.CompilerParams(vmem_limit_bytes=24 << 20),
        cost_estimate=pl.CostEstimate(flops=5 * 10**8, bytes_accessed=20 * 10**6, transcendentals=0),
        name=f"correct{n}",
    )(place, received, strength, atoms, masked, right if n in EARLY else right[:, :8, :LANES], before)


LINES_STEP = 4


def lines_kernel(n, field, left, right, *rest):
    *chunks, half_done, turned, sems = rest[-3 - len(CHUNKS) :]
    step = pl.program_id(0)
    last = step == pl.num_programs(0) - 1
    rows = turned.reshape(GROUPS, 2, PLANES * 16, LANES)

    def x_lines(z, y, real, imag):
        both = propagate_rows(left, jnp.concatenate(real, axis=1), jnp.concatenate(imag, axis=1))
        for c in range(2):
            for k in range(2):
                for d in range(GROUPS):
                    tile = both[c][d * 8 : d * 8 + 8, k * LANES : (k + 1) * LANES]
                    rows[d, z, pl.ds(c * 8 + y + k, 8, stride=16), :] = tile

    def copies(z):
        begin = 0
        for k, (chunk, planes) in enumerate(zip(chunks, CHUNKS)):
            part = turned.at[:, z, pl.ds(begin, planes)]
            yield pltpu.make_async_copy(part, chunk.at[:, :, n, z], sems.at[z, k])
            begin += planes

    if n in EARLY:
        for z in range(2):
            for k in range(0, LINES_STEP, 2):
                parts = ([field[:, k + j, c, z].reshape(SIZE, LANES) for j in range(2)] for c in range(2))
                x_lines(z, step * LINES_STEP + k, *parts)

            @pl.when(last)
            def _():
                for copy in copies(z):
                    copy.start()

    else:
        for k in range(LINES_STEP):
            real, imag = ([field[:, k, c, z].reshape(SIZE, LANES) for z in range(2)] for c in range(2))
            both = propagate_lanes(right, real, imag)
            y = step * LINES_STEP + k
            for c in range(2):
                for z in range(2):
                    half_done[c, z, y] = both[c][:, z * LANES : (z + 1) * LANES]

        @pl.when(last)
        def _():
            for z in range(2):
                for y in range(0, 8, 2):
                    x_lines(z, y, *([half_done[c, z, y + j] for j in range(2)] for c in range(2)))
                for copy in copies(z):
                    copy.start()

    @pl.when(last)
    def _():
        for z in range(2):
            for copy in copies(z):
                copy.wait()


def lines(n, field, left, right, before=(), first=()):
    hbm = pl.BlockSpec(memory_space=pltpu.HBM)
    return pl.pallas_call(
        functools.partial(lines_kernel, n),
        grid=(8 // LINES_STEP,),
        out_shape=tuple(
            jax.ShapeDtypeStruct((GROUPS, planes, ORBS, 2, 16, LANES), jnp.float32) for planes in CHUNKS
        ),
        in_specs=[
            pl.BlockSpec((GROUPS, LINES_STEP, 2, 2, 8, LANES), lambda i: (0, i, 0, 0, 0, 0)),
            pl.BlockSpec(left.shape, lambda i: (0, 0, 0)),
            pl.BlockSpec(right.shape, lambda i: (0, 0, 0)),
            *[hbm for _ in (*before, *first)],
        ],
        out_specs=tuple(hbm for _ in CHUNKS),
        scratch_shapes=[
            pltpu.VMEM((2, 2, 8, SIZE, LANES), jnp.float32),
            pltpu.VMEM((GROUPS, 2, PLANES, 16, LANES), jnp.float32),
            pltpu.SemaphoreType.DMA((2, len(CHUNKS))),
        ],
        input_output_aliases={3 + k: k for k in range(len(before))},
        compiler_params=pltpu.CompilerParams(vmem_limit_bytes=VMEM),
        cost_estimate=pl.CostEstimate(flops=5 * 10**9, bytes_accessed=10 * 10**6, transcendentals=0),
        name=f"lines{n}",
    )(field.reshape(GROUPS, 8, 2, 2, 8, LANES), left, right, *before, *first)


def finish_kernel(halves, band, field, potential, left, *rest):
    out, *pieces, whole = rest[-2 - BANDS * halves :]
    cosine, sine = cos_sin((0.5 * TIME_STEP) * potential[0])
    total = None
    for n in range(ORBS):
        real, imag = (
            jnp.concatenate([field[:, 0, n, z, c].reshape(SIZE, LANES) for z in range(2)], axis=1) for c in range(2)
        )
        real, imag = propagate_rows(left, real, imag)
        real, imag = cosine * real + sine * imag, cosine * imag - sine * real
        out[0, n, 0] = real
        out[1, n, 0] = imag
        square = real * real + imag * imag
        total = square if total is None else total + square
    whole[...] = total
    rows = SIZE // BANDS // halves
    for k, piece in enumerate(pieces):
        begin = (band[0] + k // halves) % BANDS * halves + k % halves
        piece[0] = whole[pl.ds(pl.multiple_of(begin * rows, rows), rows), :]


def finish(planes, begin, halves, band, field, potential, left, before=(), first=()):
    rows = SIZE // BANDS // halves
    return pl.pallas_call(
        functools.partial(finish_kernel, halves),
        grid=(planes,),
        out_shape=(
            jax.ShapeDtypeStruct((2, ORBS, PLANES, SIZE, SIZE), jnp.float32),
            *[jax.ShapeDtypeStruct((planes, rows, SIZE), jnp.float32) for _ in range(BANDS * halves)],
        ),
        in_specs=[
            pl.BlockSpec(memory_space=pltpu.SMEM),
            pl.BlockSpec((GROUPS, 1, ORBS, 2, 2, 8, LANES), lambda i: (0, i, 0, 0, 0, 0, 0)),
            pl.BlockSpec((1, SIZE, SIZE), lambda i: (i + begin, 0, 0)),
            pl.BlockSpec(left.shape, lambda i: (0, 0, 0)),
            *[pl.BlockSpec(memory_space=pl.ANY) for _ in (*before, *first)],
        ],
        out_specs=(
            pl.BlockSpec((2, ORBS, 1, SIZE, SIZE), lambda i: (0, 0, i + begin, 0, 0)),
            *[pl.BlockSpec((1, rows, SIZE), lambda i: (i, 0, 0)) for _ in range(BANDS * halves)],
        ),
        scratch_shapes=[pltpu.VMEM((SIZE, SIZE), jnp.float32)],
        input_output_aliases={4 + k: k for k in range(len(before))},
        compiler_params=pltpu.CompilerParams(vmem_limit_bytes=VMEM),
        cost_estimate=pl.CostEstimate(flops=10**9 * planes, bytes_accessed=3 * 10**6 * planes, transcendentals=0),
        name=f"finish{begin}",
    )(band, field.reshape(GROUPS, planes, ORBS, 2, 2, 8, LANES), potential, left, *before, *first)


def collect_kernel(owners, band, *refs):
    out, mark = refs[-2:]
    mark[...] = jnp.zeros_like(mark)
    rows = SIZE // BANDS
    for piece, (owner, offset) in zip(refs, owners):
        row = pl.multiple_of((band[0] + owner) % BANDS * rows, rows)
        out[0, pl.ds(pl.multiple_of(row + offset, rows // 2), piece.shape[1]), :] = piece[0]


def collect(begin, band, pieces, owners, *before):
    return pl.pallas_call(
        functools.partial(collect_kernel, owners),
        grid=(pieces[0].shape[0],),
        out_shape=(
            jax.ShapeDtypeStruct((PLANES, SIZE, SIZE), jnp.float32),
            jax.ShapeDtypeStruct((8, LANES), jnp.float32),
        ),
        in_specs=[
            pl.BlockSpec(memory_space=pltpu.SMEM),
            *[pl.BlockSpec((1, piece.shape[1], SIZE), lambda i: (i, 0, 0)) for piece in pieces],
            *[pl.BlockSpec(memory_space=pltpu.HBM) for _ in before],
        ],
        out_specs=(
            pl.BlockSpec((1, SIZE, SIZE), lambda i: (i + begin, 0, 0)),
            pl.BlockSpec((8, LANES), lambda i: (0, 0)),
        ),
        input_output_aliases={1 + len(pieces) + k: k for k in range(len(before))},
        compiler_params=pltpu.CompilerParams(vmem_limit_bytes=VMEM if begin == 0 else 16 << 20),
        cost_estimate=pl.CostEstimate(flops=0, bytes_accessed=3 * 10**6, transcendentals=0),
        name=f"collect{begin}",
    )(band, *pieces, *before)


def onward(array, steps):
    return lax.ppermute(array, "band", [(b, (b + steps) % BANDS) for b in range(BANDS)])


def ring_reduce(pieces):
    own_low, own_high, next_low, next_high, across_low, across_high, last_low, last_high = pieces
    from_last = onward(across_low, 1)
    from_next = onward(across_high, 3)
    high = own_high + onward(next_high, 1)
    low = own_low + onward(last_low, 3)
    return low + onward(next_low + from_last, 1), high + onward(last_high + from_next, 3)


def ring_gather(low, high):
    last_low, next_high = onward(low, 1), onward(high, 3)
    last_high, next_low = onward(high, 1), onward(low, 3)
    pieces = low, high, last_low, last_high, next_low, next_high, onward(last_low, 1), onward(next_high, 3)
    half = SIZE // BANDS // 2
    return pieces, tuple((owner, offset) for owner in (0, 3, 1, 2) for offset in (0, half))


def add_kernel(own, from_last, across, from_next, *rest):
    rest[-1][...] = own[...] + from_last[...] + across[...] + from_next[...]


def direct_reduce(pieces, first):
    parts = [pieces[0], *[onward(pieces[k], k) for k in range(1, BANDS)]]
    return pl.pallas_call(
        add_kernel,
        out_shape=jax.ShapeDtypeStruct(pieces[0].shape, jnp.float32),
        in_specs=[
            *[pl.BlockSpec(memory_space=pltpu.VMEM) for _ in parts],
            *[pl.BlockSpec(memory_space=pltpu.HBM) for _ in first],
        ],
        out_specs=pl.BlockSpec(memory_space=pltpu.VMEM),
        compiler_params=pltpu.CompilerParams(vmem_limit_bytes=16 << 20),
        cost_estimate=pl.CostEstimate(flops=10**6, bytes_accessed=10**6, transcendentals=0),
        name="add",
    )(*parts, *first)


def direct_gather(total):
    return (total, *[onward(total, k) for k in range(1, BANDS)]), ((0, 0), (3, 0), (2, 0), (1, 0))


def exchange(array):
    return lax.all_to_all(array, "grid", split_axis=0, concat_axis=0, tiled=True)


def body(left, right, orbitals, potential, projectors, entry_atom, entry_block, entry_count, owner_slot, strength):
    atom_ids = jnp.arange(ATOMS, dtype=jnp.int32)
    rows = PLANES * SIZE
    band = lax.axis_index("band").astype(jnp.int32).reshape(1)
    sent, masked = project(
        orbitals.reshape(2 * ORBS, rows, SIZE), potential.reshape(rows, SIZE), projectors,
        entry_atom, entry_block, entry_count, owner_slot,
    )
    received = exchange(sent)
    x, y, z = entry_block // 512, (entry_block // 2) % SIZE, entry_block % 2
    place = y * 32 + z * 8 + x
    in_slot = owner_slot[:, None] == atom_ids[None, :]
    strength_atom = jnp.sum(jnp.where(in_slot, strength[None, :], 0.0), axis=1).reshape(4, LANES)
    atoms = entry_atom.reshape(1, ENTRIES)
    pencils, sent = [], ()
    for n in range(ORBS):
        shifted = shift(n, orbitals, potential, *sent)
        fixed = correct(n, place, received, strength_atom, atoms, masked, right, shifted)
        pencils.append(exchange(fixed.reshape(GROUPS, 256, LANES)))
        sent = (fixed,)
    mine = jnp.sum(received[:, 16:], axis=0)
    mine = jnp.concatenate([mine[:, :OWNED], mine[:, OWNED : 2 * OWNED]], axis=0).reshape(4, 2 * ORBS, OWNED)
    strength_mine = lax.dynamic_slice_in_dim(strength, lax.axis_index("grid") * OWNED, OWNED)
    forces = -2.0 * strength_mine * jnp.sum(mine[0][None] * mine[1:], axis=1)
    forces = sum([onward(forces, k) for k in range(1, BANDS)], forces)

    back = lines(0, pencils[0], left, right)
    back = lines(1, pencils[1], left, right, back, (forces,))
    out, density, ready, marks, begin = (), (), (), (), 0
    for k, planes in enumerate(CHUNKS):
        field = exchange(back[k])
        made, *pieces = finish(planes, begin, 2 if k == 0 else 1, band, field, potential, left, out, ready)
        out = (made,)
        if k == 0:
            sums, owners = ring_gather(*ring_reduce(pieces))
            ready = sums[2:]
        else:
            sums, owners = direct_gather(direct_reduce(pieces, marks))
        made, mark = collect(begin, band, sums, owners, *density)
        density, marks = (made,), (mark,)
        begin += planes
    return out[0], density[0], forces


def solution(mesh):
    left, right = propagator_tables()
    in_specs = (
        P(None, "band", "grid", None, None),
        P("grid", None, None),
        P(None, "grid", None),
        P("grid"),
        P("grid"),
        P("grid"),
        P(),
        P(),
    )
    out_specs = (P(None, "band", "grid", None, None), P("grid", None, None), P(None, "grid"))

    def run(*args):
        return body(jnp.asarray(left), jnp.asarray(right), *args)

    return jax.shard_map(run, mesh=mesh, in_specs=in_specs, out_specs=out_specs, check_vma=False)
```
